256 devices in a mesh: ad: 32 (over x, z), tp: 8 (over y, core).
Axes of the slice: x: 4, y: 4, z: 8, core: 2. Of those that a mesh axis runs over, the one named last changes fastest.
Arguments:
- tokens: bfloat16 [49152, 8192], P('ad', 'tp'), may hold values from -6 to 6
- key_value_weight: bfloat16 [2, 8192, 1024], P(None, 'tp'), may hold values from -0.09375 to 0.09375
- adapter_down_weights: bfloat16 [128, 8192, 128], P('ad', 'tp'), may hold values from -0.0625 to 0.0625
- adapter_up_weights: bfloat16 [128, 2, 64, 1024], P('ad', None, None, 'tp'), may hold values from -0.75 to 0.75
- token_adapter_ident: int32 [49152, 1], P('ad'), may hold values from 0 to 127; in each aligned block of 1536 rows (0 to 1535, 1536 to 3071, ...) at most 18 rows name the same one
- adapter_storage_slot: int32 [128], replicated, may hold values from 0 to 127, each once
Outputs:
- projected: bfloat16 [49152, 2, 1024], P('ad', None, 'tp')
The draws below stay inside these ranges and needn't reach their ends.
Inputs may be any that keep to these rules, and one draw needn't show every extreme that they name: `token_adapter_ident`: among the rows of one device no adapter id stands more than 18 times, and some id stands exactly 18 times. A permutation: adapter a is stored at position adapter_storage_slot[a] of adapter_down_weights and adapter_up_weights.
All inputs are finite; a program needn't handle non-finite values.
Results may differ from the reference program's by a relative error of at most 0.02.
Values may be sent and summed in bfloat16 or wider, within the bound.
No kernel may reach another device: no remote copies, remote signals or barrier semaphores. Data moves between devices by JAX's collectives and lax.ppermute only.
A program may use at most 128 MiB of HBM per device.

```python
import math
import jax
import jax.numpy as jnp
import numpy as np
from jax import lax

MODEL_WIDTH = 8192
KEY_VALUE_WIDTH = 1024
ADAPTER_RANK = 64
TOK_DEV = 1536
ADAPTER_TOTAL = 128
MOST = 18
TOKENS = 49152
N_AD = 32
N_TP = 8


def strengthened(array, rng, source, target, blocks, factor):
    owner, partner = [(jnp.arange(array.shape[dim]) // (array.shape[dim] // blocks)).reshape([-1 if axis == dim else 1 for axis in range(array.ndim)]) for dim in (source, target)]
    chosen = jax.random.permutation(rng, blocks)[partner]
    strong = (owner == chosen) | (owner == (partner + blocks // 2) % blocks)
    return jnp.where(strong, factor * array, array)


def levels(key, dims, shards, least, top_value):
    loudness, own = 1.0, jax.random.fold_in(key, 6)
    for dim, shards_of in shards:
        heights = jnp.exp(jax.random.uniform(jax.random.fold_in(own, dim), (shards_of,), jnp.float32, least / len(shards), top_value / len(shards)))
        loudness = loudness * jnp.repeat(heights, dims[dim] // shards_of).reshape([-1 if axis == dim else 1 for axis in range(len(dims))])
    return loudness


def assign_block(rng, own, number, rows, number_of, top, bound, slope):
    sequence = jax.random.permutation(rng, number_of)
    crowded, common = portions_of(number_of, rows * top, bound, slope, True), portions_of(number_of, rows * top, bound, slope, False)
    places = jnp.arange(number_of)

    def named(sizes, offset_by):
        used = int((sizes > 0).sum())
        fixed = max(1, used // 4)
        passed = fixed + (places - fixed + offset_by * (used - fixed)) % max(1, number_of - fixed)
        return jnp.zeros((number_of,), jnp.int32).at[sequence[jnp.where(places < fixed, places, passed)]].set(jnp.asarray(sizes, jnp.int32))

    sizes = jnp.where(number % 4 == 0, named(crowded, number // 4), named(common, number - number // 4 - 1))
    mixed = jax.random.permutation(jax.random.fold_in(own, 3), number_of)
    donor, taker = mixed[0:number_of // 2 * 2:2], mixed[1:number_of // 2 * 2:2]
    margin = jnp.minimum(sizes[donor] - 1, bound - sizes[taker]) // 2
    margin = jnp.where((donor == sequence[0]) | (taker == sequence[0]) | (sizes[taker] == 0), 0, jnp.maximum(margin, 0))
    passed = jax.random.randint(jax.random.fold_in(own, 4), (number_of // 2,), 0, 1 << 20) % (margin + 1)
    sizes = sizes.at[donor].add(-passed).at[taker].add(passed)
    members = jnp.searchsorted(jnp.cumsum(sizes), jnp.arange(rows * top), side="right").astype(jnp.int32)
    grid = members.reshape(top, rows).T
    grid = grid[jax.random.permutation(jax.random.fold_in(own, 1), rows)]
    offset_by = jax.random.randint(jax.random.fold_in(own, 2), (rows, 1), 0, top)
    return jnp.take_along_axis(grid, (jnp.arange(top)[None, :] + offset_by) % top, axis=1)


def portions_of(number_of, total, limit, lean, full):
    loads = [(1 << 20) // math.isqrt(grade ** lean) + 1 for grade in range(1, number_of + 1)]
    largest = limit if full else min(limit, max(-(-total // number_of), total * loads[0] // sum(loads)))
    least = 1 if total - largest >= number_of - 1 else 0
    given, spare = [largest] + [least] * (number_of - 1), total - largest - least * (number_of - 1)
    while spare > 0:
        movable = [i for i in range(1, number_of) if given[i] < largest] or [i for i in range(1, number_of) if given[i] < limit]
        pool, remaining = sum([loads[i] for i in movable]), spare
        for i in movable:
            extra = min(limit - given[i], max(1, remaining * loads[i] // pool), spare)
            given[i] = given[i] + extra
            spare = spare - extra
    return np.array(given)


def scatter_about(stream_key, dims, spread, limit, pieces=(), kind=jnp.bfloat16):
    result = spread * jax.random.normal(stream_key, dims, jnp.float32)
    if pieces:
        result = result * levels(stream_key, dims, pieces, -0.22, 0.18)
    return jnp.clip(result, -limit, limit).astype(kind)


def bell_draw_with(own_key, dims, deviation, most, split, heavy, kind=jnp.bfloat16):
    array = deviation * jax.random.normal(own_key, dims, jnp.float32)
    if split:
        array = array * levels(own_key, dims, split, -0.22, 0.18)
    return jnp.clip(strengthened(array, jax.random.fold_in(own_key, 3), *heavy), -most, most).astype(kind)


def setup_inputs(seed: int = 0) -> dict:
    key_list = jax.random.split(jax.random.key(seed), 7)
    tokens = scatter_about(key_list[0], (TOKENS, MODEL_WIDTH), 1.0, 6.0, ((0, 32), (1, 8)))
    key_value_weight = bell_draw_with(key_list[1], (2, MODEL_WIDTH, KEY_VALUE_WIDTH), MODEL_WIDTH ** -0.5, 0.09375, ((1, 8),), (1, 2, 8, 2.0))
    adapter_down_weights = scatter_about(key_list[2], (ADAPTER_TOTAL, MODEL_WIDTH, 2 * ADAPTER_RANK), MODEL_WIDTH ** -0.5, 0.0625, ((0, 32), (1, 8)))
    adapter_up_weights = scatter_about(key_list[3], (ADAPTER_TOTAL, 2, ADAPTER_RANK, KEY_VALUE_WIDTH), ADAPTER_RANK ** -0.5, 0.75, ((0, 32), (3, 8)))
    token_adapter_ident_keys = jax.random.split(jax.random.fold_in(key_list[4], 1), TOKENS // TOK_DEV)
    token_adapter_ident_turns = jax.random.permutation(jax.random.fold_in(key_list[4], 3), TOKENS // TOK_DEV)
    token_adapter_ident = jax.vmap(lambda own, number: assign_block(jax.random.fold_in(key_list[4], 2), own, number, TOK_DEV, ADAPTER_TOTAL, 1, MOST, 2))(token_adapter_ident_keys, token_adapter_ident_turns).reshape((TOKENS, 1))
    adapter_storage_slot = jax.random.permutation(key_list[5], ADAPTER_TOTAL).astype(jnp.int32)
    return {"tokens": tokens, "key_value_weight": key_value_weight, "adapter_down_weights": adapter_down_weights, "adapter_up_weights": adapter_up_weights, "token_adapter_ident": token_adapter_ident, "adapter_storage_slot": adapter_storage_slot}


def base_output(tokens, key_value_weight):
    block_width = MODEL_WIDTH // N_TP

    def one_block(running, block_index):
        features = lax.dynamic_slice_in_dim(tokens, block_index * block_width, block_width, 1).astype(jnp.float32)
        weights = lax.dynamic_slice_in_dim(key_value_weight, block_index * block_width, block_width, 1).astype(jnp.float32)
        product = jnp.einsum('tf,cfk->tck', features, weights)
        rounded = lax.optimization_barrier(product.astype(jnp.bfloat16))
        return running + rounded.astype(jnp.float32), None

    initial = jnp.zeros((TOKENS, 2, KEY_VALUE_WIDTH), jnp.float32)
    return lax.scan(one_block, initial, jnp.arange(N_TP, dtype=jnp.int32))[0]


def adapter_result_rows(tokens, adapter_down_weights, adapter_up_weights, token_adapter_ident, adapter_storage_slot):
    adapter_ids = token_adapter_ident[:, 0].astype(jnp.int32)
    sort_order = jnp.argsort(adapter_ids, stable=True).astype(jnp.int32)
    sorted_ids = adapter_ids[sort_order]
    catalog = jnp.arange(ADAPTER_TOTAL, dtype=jnp.int32)
    counts = jnp.sum((adapter_ids[None, :] == catalog[:, None]).astype(jnp.int32), axis=1)
    starts = (jnp.cumsum(counts) - counts).astype(jnp.int32)
    capacity = N_AD * MOST
    padded = jnp.concatenate([tokens[sort_order], jnp.zeros((capacity, MODEL_WIDTH), jnp.bfloat16)], axis=0)

    def one_adapter(adapter):
        first_row = starts[adapter]
        rows = lax.dynamic_slice_in_dim(padded, first_row, capacity, 0)
        kept_adapters = adapter_storage_slot[adapter]
        down_matrix = adapter_down_weights[kept_adapters]
        up_matrix = adapter_up_weights[kept_adapters]
        reduced_rows = jnp.dot(rows, down_matrix, preferred_element_type=jnp.float32).astype(jnp.bfloat16)
        halves = reduced_rows.reshape(capacity, 2, ADAPTER_RANK).astype(jnp.float32)
        lowrank_delta = jnp.einsum('rcq,cqk->rck', halves, up_matrix.astype(jnp.float32))
        return lowrank_delta.astype(jnp.bfloat16)

    deltas = lax.map(one_adapter, catalog)
    position = jnp.arange(TOKENS, dtype=jnp.int32) - starts[sorted_ids]
    sorted_update = deltas[sorted_ids, position]
    return jnp.zeros((TOKENS, 2, KEY_VALUE_WIDTH), jnp.bfloat16).at[sort_order].set(sorted_update)


def reference(tokens, key_value_weight, adapter_down_weights, adapter_up_weights, token_adapter_ident, adapter_storage_slot):
    base_out = base_output(tokens, key_value_weight)
    lowrank_delta = adapter_result_rows(tokens, adapter_down_weights, adapter_up_weights, token_adapter_ident, adapter_storage_slot)
    return (base_out + lowrank_delta.astype(jnp.float32)).astype(jnp.bfloat16)
```

```python
import functools

import jax
import jax.numpy as jnp
from jax import lax
from jax.experimental import pallas as pl
from jax.experimental.pallas import tpu as pltpu
from jax.sharding import PartitionSpec as P

F32 = jnp.float32
BF16 = jnp.bfloat16
I32 = jnp.int32

NX, NZ = 4, 8
NY = 4
LOCAL = 4
CAP = 18
BLOCK = LOCAL * CAP
WIDE = 80

ORDER = (0, 7, 1, 6, 2, 5, 3, 4)
CHUNKS = ((0, 368, (0, 7, 1, 6, 2)), (368, 144, (5, 3)), (512, 80, (4,)))
ROWS = 592
COST = {
    "route": 3, "pack": 11, "base": 11, "gather": 7, "finish": 6,
    "shrink": (20, 4, 40), "expand": (20, 3, 30),
}
VMEM = 56 * 1024 * 1024


def iota(shape, dim):
    return lax.broadcasted_iota(I32, shape, dim)


def params(*semantics):
    if semantics:
        return pltpu.CompilerParams(vmem_limit_bytes=VMEM, dimension_semantics=semantics)
    return pltpu.CompilerParams(vmem_limit_bytes=VMEM)


def cost(micros):
    return pl.CostEstimate(
        flops=int(micros * 1.1e9), bytes_accessed=1000, transcendentals=0
    )


def whole():
    return pl.BlockSpec(memory_space=pltpu.VMEM)


def scalars():
    return pl.BlockSpec(memory_space=pltpu.SMEM)


def route_kernel(place_ref, ids_ref, store_ref, row_ref, col_ref):
    x, z = place_ref[0], place_ref[1]
    count = ids_ref.shape[1]
    ids = jnp.broadcast_to(ids_ref[...], (128, count))
    ids_down = ids.T
    store = jnp.broadcast_to(store_ref[...], (128, 128)).T
    for j in range(count // 128):
        mine = ids[:, j * 128 : (j + 1) * 128]
        placed = jnp.sum(
            jnp.where(mine == iota((128, 128), 0), store, 0), axis=0, keepdims=True
        )
        seen = (j + 1) * 128
        same = (ids_down[:seen] == mine[:1]) & (
            iota((seen, 128), 0) < iota((seen, 128), 1) + j * 128
        )
        ordinal = jnp.sum(same.astype(I32), axis=0, keepdims=True)
        owner = placed >> 2
        east = ((owner >> 3) - x) & 3
        north = ((owner & 7) - z) & 7
        start = jnp.zeros_like(owner)
        for first, _, blocks in CHUNKS:
            for k, offset in enumerate(blocks):
                start = jnp.where(north == offset, first + k * BLOCK, start)
        row_ref[:, j * 128 : (j + 1) * 128] = (
            east * ROWS + start + (placed & 3) * CAP + ordinal
        )
    col_ref[...] = jnp.broadcast_to(row_ref[...], (128, count)).T


def route(place, ids, store):
    count = ids.shape[1]
    return pl.pallas_call(
        route_kernel,
        out_shape=(
            jax.ShapeDtypeStruct((1, count), I32),
            jax.ShapeDtypeStruct((count, 128), I32),
        ),
        in_specs=[scalars(), whole(), whole()],
        out_specs=(whole(), whole()),
        compiler_params=params(),
        cost_estimate=cost(COST['route']),
        name="route",
    )(place, ids, store)


def pack_kernel(row_ref, tok_ref, *refs):
    outs, hot = refs[:NX], refs[NX]

    @pl.when(pl.program_id(0) == 0)
    def _():
        count = row_ref.shape[1]
        rows = row_ref[...]
        for e in range(NX):
            hot[e] = (rows == iota((ROWS, count), 0) + e * ROWS).astype(BF16)

    for e in range(NX):
        outs[e][...] = jnp.dot(
            hot[e], tok_ref[...], preferred_element_type=F32
        ).astype(BF16)


def pack(row, tokens):
    count, width = tokens.shape
    step = 256
    return pl.pallas_call(
        pack_kernel,
        grid=(width // step,),
        out_shape=[jax.ShapeDtypeStruct((ROWS, width), BF16)] * NX,
        in_specs=[
            pl.BlockSpec((1, count), lambda i: (0, 0)),
            pl.BlockSpec((count, step), lambda i: (0, i)),
        ],
        out_specs=[pl.BlockSpec((ROWS, step), lambda i: (0, i))] * NX,
        scratch_shapes=[pltpu.VMEM((NX, ROWS, count), BF16)],
        compiler_params=params("arbitrary"),
        cost_estimate=cost(COST['pack']),
        name="pack",
    )(row, tokens)


def base_kernel(tok_ref, w_ref, _, out_ref):
    parts = out_ref.shape[0]
    for c in range(2):
        y = jnp.dot(tok_ref[...], w_ref[c], preferred_element_type=F32).astype(BF16)
        for p in range(parts):
            out_ref[p, :, c * 128 : (c + 1) * 128] = y[:, p * 128 : (p + 1) * 128]


def base(tokens, weight, parts, earlier):
    count, width = tokens.shape
    out_width = weight.shape[2]
    step = 256
    return pl.pallas_call(
        base_kernel,
        grid=(count // step,),
        out_shape=jax.ShapeDtypeStruct((parts, count, 256), BF16),
        in_specs=[
            pl.BlockSpec((step, width), lambda i: (i, 0)),
            pl.BlockSpec(weight.shape, lambda i: (0, 0, 0)),
            pl.BlockSpec(memory_space=pl.ANY),
        ],
        out_specs=pl.BlockSpec((parts, step, 256), lambda i: (0, i, 0)),
        compiler_params=params("arbitrary"),
        cost_estimate=cost(COST['base']),
        name="base",
    )(tokens, weight, earlier)


def spans(blocks):
    for k in range(len(blocks)):
        low = k * BLOCK // 16 * 16
        yield k, low


def adapter_of(k, low):
    row = iota((WIDE, 1), 0) + (low - k * BLOCK)
    which = jnp.full((WIDE, 1), -1, I32)
    for a in range(LOCAL):
        which = jnp.where((row >= a * CAP) & (row < (a + 1) * CAP), a, which)
    return jnp.concatenate([which] * NX, axis=0)


def shrink_kernel(blocks, pieces, *refs):
    xs, ws = refs[:NX], refs[NX : NX + len(pieces)]
    out_ref, total = refs[-2], refs[-1]
    total[...] = jnp.zeros_like(total)
    for k, low in spans(blocks):
        panels = [
            w[a] for w, (block, n) in zip(ws, pieces, strict=True) if block == k for a in range(n)
        ]
        rows = jnp.concatenate([x[low : low + WIDE, :] for x in xs], axis=0)
        y = jnp.dot(rows, jnp.concatenate(panels, axis=1), preferred_element_type=F32)
        which = adapter_of(k, low)
        kept = jnp.zeros((NX * WIDE, 128), F32)
        for a in range(LOCAL):
            kept = kept + jnp.where(which == a, y[:, a * 128 : (a + 1) * 128], 0.0)
        for e in range(NX):
            total[e, low : low + WIDE, :] += kept[e * WIDE : (e + 1) * WIDE]
    out_ref[...] = total[...].astype(BF16)


def shrink(chunk, xs, panels):
    first, size, blocks = chunk
    pieces = tuple((k, w.shape[0]) for k, w in panels)
    width = xs[0].shape[1]
    return pl.pallas_call(
        functools.partial(shrink_kernel, blocks, pieces),
        grid=(1,),
        out_shape=jax.ShapeDtypeStruct((NX, size, 128), BF16),
        in_specs=[
            pl.BlockSpec((pl.Element(size), pl.Element(width)), lambda i: (first, 0))
        ] * NX
        + [pl.BlockSpec(w.shape, lambda i: (0, 0, 0)) for _, w in panels],
        out_specs=pl.BlockSpec((NX, size, 128), lambda i: (0, 0, 0)),
        scratch_shapes=[pltpu.VMEM((NX, size, 128), F32)],
        compiler_params=params("arbitrary"),
        cost_estimate=cost(COST['shrink'][CHUNKS.index(chunk)]),
        name="shrink",
    )(*xs, *[w for _, w in panels])


def expand_kernel(blocks, place_ref, *refs):
    parts, up_ref, outs = refs[:NY], refs[NY], refs[NY + 1 : NY + 1 + NX]
    wide_up, total = refs[-2], refs[-1]
    z = place_ref[1]
    shrunk = parts[0][...].astype(F32)
    for part in parts[1:]:
        shrunk = shrunk + part[...].astype(F32)
    shrunk = shrunk.astype(BF16)
    wide_up[...] = jnp.zeros_like(wide_up)
    total[...] = jnp.zeros_like(total)
    for k, low in spans(blocks):
        owner = ((z + blocks[k]) & (NZ - 1)) * LOCAL
        for a in range(LOCAL):
            for c in range(2):
                wide_up[a * 128 + c * 64 : a * 128 + c * 64 + 64, c * 128 : (c + 1) * 128] = (
                    up_ref[owner + a, c]
                )
        rows = jnp.concatenate([shrunk[e, low : low + WIDE] for e in range(NX)], axis=0)
        which = adapter_of(k, low)
        lhs = jnp.concatenate(
            [jnp.where(which == a, rows, jnp.zeros_like(rows)) for a in range(LOCAL)], axis=1
        )
        y = jnp.dot(lhs, wide_up[...], preferred_element_type=F32)
        for e in range(NX):
            total[e, low : low + WIDE, :] += y[e * WIDE : (e + 1) * WIDE]
    for e in range(NX):
        outs[e][...] = total[e].astype(BF16)


def expand(chunk, place, parts, up):
    _, size, blocks = chunk
    return pl.pallas_call(
        functools.partial(expand_kernel, blocks),
        out_shape=[jax.ShapeDtypeStruct((size, 256), BF16)] * NX,
        in_specs=[scalars()] + [whole()] * (NY + 1),
        out_specs=[whole()] * NX,
        scratch_shapes=[pltpu.VMEM((LOCAL * 128, 256), BF16), pltpu.VMEM((NX, size, 256), F32)],
        compiler_params=params(),
        cost_estimate=cost(COST['expand'][CHUNKS.index(chunk)]),
        name="expand",
    )(place, *parts, up)


def picked(slot, chunk, deltas):
    first, size, _ = chunk
    total = jnp.zeros((slot.shape[0], 256), F32)
    for e in range(NX):
        hot = (slot == iota((slot.shape[0], size), 1) + (e * ROWS + first)).astype(BF16)
        total = total + jnp.dot(hot, deltas[e][...], preferred_element_type=F32)
    return total


def gather_kernel(chunks, col_ref, base_ref, *refs):
    slot = col_ref[:, :1]
    total = base_ref[...].astype(F32)
    for n, chunk in enumerate(chunks):
        total = total + picked(slot, chunk, refs[n * NX : (n + 1) * NX])
    refs[-1][...] = total


def gather(chunks, col, summed, deltas):
    count = col.shape[0]
    step = 256
    return pl.pallas_call(
        functools.partial(gather_kernel, chunks),
        grid=(count // step,),
        out_shape=jax.ShapeDtypeStruct((count, 256), F32),
        in_specs=[
            pl.BlockSpec((step, 128), lambda i: (i, 0)),
            pl.BlockSpec((step, 256), lambda i: (i, 0)),
        ]
        + [pl.BlockSpec(d.shape, lambda i: (0, 0)) for d in deltas],
        out_specs=pl.BlockSpec((step, 256), lambda i: (i, 0)),
        compiler_params=params("arbitrary"),
        cost_estimate=cost(COST['gather']),
        name="gather",
    )(col, summed, *deltas)


def finish_kernel(chunk, col_ref, total_ref, *refs):
    out_ref, both = refs[-2], refs[-1]
    rows = col_ref.shape[0]
    total = total_ref[...] + picked(col_ref[:, :1], chunk, refs[:NX])
    both[pl.ds(0, rows, stride=2), :] = total[:, :128]
    both[pl.ds(1, rows, stride=2), :] = total[:, 128:]
    out_ref[...] = both[...].astype(BF16)


def finish(chunk, col, total, deltas):
    count = col.shape[0]
    step = 256
    return pl.pallas_call(
        functools.partial(finish_kernel, chunk),
        grid=(count // step,),
        out_shape=jax.ShapeDtypeStruct((2 * count, 128), BF16),
        in_specs=[
            pl.BlockSpec((step, 128), lambda i: (i, 0)),
            pl.BlockSpec((step, 256), lambda i: (i, 0)),
        ]
        + [pl.BlockSpec(d.shape, lambda i: (0, 0)) for d in deltas],
        out_specs=pl.BlockSpec((2 * step, 128), lambda i: (i, 0)),
        scratch_shapes=[pltpu.VMEM((2 * step, 128), F32)],
        compiler_params=params("arbitrary"),
        cost_estimate=cost(COST['finish']),
        name="finish",
    )(col, total, *deltas)


def along_z(array, d):
    pairs = [(x * NZ + z, x * NZ + (z + d) % NZ) for x in range(NX) for z in range(NZ)]
    return lax.ppermute(array, "ad", pairs)


def along_x(array, d):
    pairs = [(x * NZ + z, (x + d) % NX * NZ + z) for x in range(NX) for z in range(NZ)]
    return lax.ppermute(array, "ad", pairs)


def along_y(array, d):
    pairs = [(y * 2 + c, (y + d) % NY * 2 + c) for y in range(NY) for c in range(2)]
    return lax.ppermute(array, "tp", pairs)


def other_core(array):
    return lax.ppermute(array, "tp", [(i, i ^ 1) for i in range(2 * NY)])


def adapter_rows(chunk, place, xs, panels, up):
    partial = shrink(chunk, xs, panels)
    chip = (partial.astype(F32) + other_core(partial).astype(F32)).astype(BF16)
    parts = [chip] + [along_y(chip, d) for d in (2, 1, 3)]
    deltas = expand(chunk, place, parts, up)
    return [deltas[0]] + [along_x(deltas[e], -e) for e in (1, 2, 3)]


def after(value, *others):
    return lax.optimization_barrier((value, *others))[0]


def body(tokens, weight, down, up, ident, store):
    index = lax.axis_index("ad")
    place = jnp.stack([index >> 3, index & 7]).astype(I32)
    groups = [[x * NZ + z for z in range(NZ)] for x in range(NX)]

    cw1, ccw1 = along_z(down, 1), along_z(down, -1)
    row, col = route(place, ident.reshape(1, -1), store.reshape(1, -1))
    packed = pack(row, tokens)
    xs = [packed[0]] + [along_x(packed[e], e) for e in (1, 2, 3)]
    ups = lax.all_gather(up, "ad", axis_index_groups=groups, tiled=True)

    partial_base = base(tokens, weight, lax.axis_size("tp"), packed[1])
    summed = lax.psum_scatter(partial_base, "tp", scatter_dimension=0, tiled=True)[0]
    cw2, ccw2 = along_z(cw1, 1), along_z(ccw1, -1)
    cw3, ccw3 = along_z(cw2, 1), along_z(ccw2, -1)
    last = (along_z(cw3[:2], 1), along_z(ccw3[2:], -1))

    a = adapter_rows(
        CHUNKS[0], place, xs, [(0, down), (1, cw1), (2, ccw1), (3, cw2), (4, ccw2)], ups
    )
    b = adapter_rows(CHUNKS[1], place, xs, [(0, cw3), (1, ccw3)], ups)
    c = adapter_rows(CHUNKS[2], place, xs, [(0, last[0]), (0, last[1])], ups)
    total = gather(CHUNKS[:2], col, summed, a + b)
    out = finish(CHUNKS[2], col, total, c)
    return out.reshape(tokens.shape[0], 2, 128)


def solution(mesh):
    return jax.shard_map(
        body,
        mesh=mesh,
        in_specs=(
            P("ad", "tp"),
            P(None, "tp", None),
            P("ad", "tp", None),
            P("ad", None, None, "tp"),
            P("ad", None),
            P(),
        ),
        out_specs=P("ad", None, "tp"),
        check_vma=False,
    )
```

```python
import functools

import jax
import jax.numpy as jnp
from jax import lax
from jax.experimental import pallas as pl
from jax.experimental.pallas import tpu as pltpu
from jax.sharding import PartitionSpec as P

F32 = jnp.float32
BF16 = jnp.bfloat16
I32 = jnp.int32

NX, NZ = 4, 8
NY = 4
LOCAL = 4
CAP = 18
BLOCK = LOCAL * CAP
WIDE = 80

NEAR = (0, 7, 1, 6, 2)
FAR = (5, 3)
OPPOSITE = 4
NEAR_ROWS = 368
FAR_ROWS = 144
ROWS = 592
LATE_ROWS = ROWS - NEAR_ROWS
START = {offset: k * BLOCK for k, offset in enumerate(NEAR)}
START.update({offset: NEAR_ROWS + k * BLOCK for k, offset in enumerate(FAR)})
START[OPPOSITE] = NEAR_ROWS + FAR_ROWS

MIB = 1024 * 1024
VMEM = 56 * MIB
COST = {
    "route": 3, "pack": 3, "base": 11, "carve": 1, "shrink_near": 1, "expand_near": 1,
    "shrink_far": 120, "shrink_late": 3, "expand_late": 30, "gather": 5, "finish": 5,
}
VMEM = 56 * 1024 * 1024


def iota(shape, dim):
    return lax.broadcasted_iota(I32, shape, dim)


def params(*semantics, limit=VMEM):
    if semantics:
        return pltpu.CompilerParams(vmem_limit_bytes=limit, dimension_semantics=semantics)
    return pltpu.CompilerParams(vmem_limit_bytes=limit)


def cost(micros):
    return pl.CostEstimate(
        flops=int(micros * 1.1e9), bytes_accessed=1000, transcendentals=0
    )


def whole():
    return pl.BlockSpec(memory_space=pltpu.VMEM)


def scalars():
    return pl.BlockSpec(memory_space=pltpu.SMEM)


def route_kernel(place_ref, ids_ref, store_ref, row_ref, col_ref):
    x, z = place_ref[0], place_ref[1]
    count = ids_ref.shape[1]
    ids = jnp.broadcast_to(ids_ref[...], (128, count))
    ids_down = ids.T
    store = jnp.broadcast_to(store_ref[...], (128, 128)).T
    for j in range(count // 128):
        mine = ids[:, j * 128 : (j + 1) * 128]
        placed = jnp.sum(
            jnp.where(mine == iota((128, 128), 0), store, 0), axis=0, keepdims=True
        )
        seen = (j + 1) * 128
        same = (ids_down[:seen] == mine[:1]) & (
            iota((seen, 128), 0) < iota((seen, 128), 1) + j * 128
        )
        ordinal = jnp.sum(same.astype(I32), axis=0, keepdims=True)
        owner = placed >> 2
        east = ((owner >> 3) - x) & 3
        north = ((owner & 7) - z) & 7
        start = jnp.zeros_like(owner)
        for offset, first in START.items():
            start = jnp.where(north == offset, first, start)
        row_ref[:, j * 128 : (j + 1) * 128] = (
            east * ROWS + start + (placed & 3) * CAP + ordinal
        )
    col_ref[...] = jnp.broadcast_to(row_ref[...], (128, count)).T


def route(place, ids, store):
    count = ids.shape[1]
    return pl.pallas_call(
        route_kernel,
        out_shape=(
            jax.ShapeDtypeStruct((1, count), I32),
            jax.ShapeDtypeStruct((count, 128), I32),
        ),
        in_specs=[scalars(), whole(), whole()],
        out_specs=(whole(), whole()),
        compiler_params=params(),
        cost_estimate=cost(COST['route']),
        name="route",
    )(place, ids, store)


def pack_kernel(e, row_ref, tok_ref, out_ref):
    hot = row_ref[...] == iota((ROWS, row_ref.shape[1]), 0) + e * ROWS
    out_ref[...] = jnp.dot(
        hot.astype(BF16), tok_ref[...], preferred_element_type=F32
    ).astype(BF16)


def pack(e, row, tokens):
    return pl.pallas_call(
        functools.partial(pack_kernel, e),
        out_shape=jax.ShapeDtypeStruct((ROWS, tokens.shape[1]), BF16),
        in_specs=[whole()] * 2,
        out_specs=whole(),
        compiler_params=params(limit=24 * MIB),
        cost_estimate=cost(COST["pack"]),
        name="pack",
    )(row, tokens)


def base_kernel(tok_ref, w_ref, *refs):
    out_ref = refs[-1]
    for p in range(out_ref.shape[0]):
        columns = slice(p * 128, (p + 1) * 128)
        both = jnp.concatenate([w_ref[0, :, columns], w_ref[1, :, columns]], axis=1)
        out_ref[p] = jnp.dot(tok_ref[...], both, preferred_element_type=F32).astype(BF16)


def base(tokens, weight, parts, *earlier):
    count, width = tokens.shape
    step = 2
    return pl.pallas_call(
        base_kernel,
        grid=(parts // step,),
        out_shape=jax.ShapeDtypeStruct((parts, count, 256), BF16),
        in_specs=[
            pl.BlockSpec((count, width), lambda i: (0, 0)),
            pl.BlockSpec((2, width, step * 128), lambda i: (0, 0, i)),
        ]
        + [pl.BlockSpec(memory_space=pl.ANY)] * len(earlier),
        out_specs=pl.BlockSpec((step, count, 256), lambda i: (i, 0, 0)),
        compiler_params=params("arbitrary"),
        cost_estimate=cost(COST["base"]),
        name="base",
    )(tokens, weight, *earlier)


def adapter_of(skip, copies):
    row = iota((WIDE, 1), 0) - skip
    which = jnp.full((WIDE, 1), -1, I32)
    for a in range(LOCAL):
        which = jnp.where((row >= a * CAP) & (row < (a + 1) * CAP), a, which)
    return jnp.concatenate([which] * copies, axis=0)


def spans(blocks):
    return [(k, k * BLOCK // 16 * 16, k * BLOCK % 16) for k in range(len(blocks))]


def shrunk_rows(rows, panel, skip, copies):
    y = jnp.dot(
        rows,
        jnp.concatenate([panel[a] for a in range(LOCAL)], axis=1),
        preferred_element_type=F32,
    )
    which = adapter_of(skip, copies)
    kept = jnp.zeros((copies * WIDE, 128), F32)
    for a in range(LOCAL):
        kept = kept + jnp.where(which == a, y[:, a * 128 : (a + 1) * 128], 0.0)
    return kept


def shrink_blocks(xs, panels, blocks, total):
    for k, low, skip in spans(blocks):
        rows = jnp.concatenate([x[low : low + WIDE, :] for x in xs], axis=0)
        kept = shrunk_rows(rows, panels[k], skip, NX)
        for e in range(NX):
            total[e, low : low + WIDE, :] += kept[e * WIDE : (e + 1) * WIDE]


def shrink_near_kernel(place_ref, *refs):
    xs, panels = refs[:NX], refs[NX : NX + len(NEAR)]
    keep_ref, send_ref, total = refs[NX + len(NEAR) + 1 :]
    total[...] = jnp.zeros_like(total)
    shrink_blocks(xs, panels, NEAR, total)
    core = place_ref[2]
    keep_ref[...] = total[pl.ds(core * 2, 2)].astype(BF16)
    send_ref[...] = total[pl.ds(2 - core * 2, 2)].astype(BF16)


def shrink_near(place, xs, panels, earlier):
    width = xs[0].shape[1]
    half = jax.ShapeDtypeStruct((2, NEAR_ROWS, 128), BF16)
    return pl.pallas_call(
        shrink_near_kernel,
        grid=(1,),
        out_shape=(half, half),
        in_specs=[scalars()]
        + [pl.BlockSpec((pl.Element(NEAR_ROWS), pl.Element(width)), lambda i: (0, 0))] * NX
        + [pl.BlockSpec(w.shape, lambda i: (0, 0, 0)) for w in panels]
        + [pl.BlockSpec(memory_space=pl.ANY)],
        out_specs=(pl.BlockSpec(half.shape, lambda i: (0, 0, 0)),) * 2,
        scratch_shapes=[pltpu.VMEM((NX, NEAR_ROWS, 128), F32)],
        compiler_params=params("arbitrary", limit=32 * MIB),
        cost_estimate=cost(COST["shrink_near"]),
        name="shrink_near",
    )(place, *xs, *panels, earlier)


def carve_kernel(*refs):
    xs, outs = refs[:NX], refs[NX:]
    for e in range(NX):
        outs[e // 2][e % 2] = xs[e][...]


def carve(xs):
    width = xs[0].shape[1]
    first = NEAR_ROWS + FAR_ROWS
    pair = jax.ShapeDtypeStruct((2, WIDE, width), BF16)
    return pl.pallas_call(
        carve_kernel,
        grid=(1,),
        out_shape=(pair, pair),
        in_specs=[pl.BlockSpec((pl.Element(WIDE), pl.Element(width)), lambda i: (first, 0))] * NX,
        out_specs=(pl.BlockSpec(pair.shape, lambda i: (0, 0, 0)),) * 2,
        compiler_params=params("arbitrary", limit=8 * MIB),
        cost_estimate=cost(COST["carve"]),
        name="carve",
    )(*xs)


def shrink_far_kernel(*refs):
    xs, panels = refs[:NX], refs[NX : NX + 2]
    out_ref, total = refs[NX + 4 :]
    total[...] = jnp.zeros_like(total)
    shrink_blocks(xs, panels, FAR, total)
    out_ref[...] = total[...].astype(BF16)


def shrink_far(xs, panels, *earlier):
    width = xs[0].shape[1]
    return pl.pallas_call(
        shrink_far_kernel,
        grid=(1,),
        out_shape=jax.ShapeDtypeStruct((NX, FAR_ROWS, 128), BF16),
        in_specs=[
            pl.BlockSpec((pl.Element(FAR_ROWS), pl.Element(width)), lambda i: (NEAR_ROWS, 0))
        ]
        * NX
        + [pl.BlockSpec(w.shape, lambda i: (0, 0, 0)) for w in panels]
        + [pl.BlockSpec(memory_space=pl.ANY)] * len(earlier),
        out_specs=pl.BlockSpec((NX, FAR_ROWS, 128), lambda i: (0, 0, 0)),
        scratch_shapes=[pltpu.VMEM((NX, FAR_ROWS, 128), F32)],
        compiler_params=params("arbitrary", limit=16 * MIB),
        cost_estimate=cost(COST["shrink_far"]),
        name="shrink_far",
    )(*xs, *panels, *earlier)


def shrink_late_kernel(far_ref, from_low, from_high, low_ref, high_ref, _, out_ref):
    out_ref[:, :FAR_ROWS, :] = far_ref[...]
    for guest, panel, first in ((from_low, high_ref, 0), (from_high, low_ref, 2)):
        kept = shrunk_rows(jnp.concatenate([guest[0], guest[1]], axis=0), panel, 0, 2)
        for e in range(2):
            out_ref[first + e, FAR_ROWS:, :] = kept[e * WIDE : (e + 1) * WIDE].astype(BF16)


def shrink_late(far, guests, panels, earlier):
    return pl.pallas_call(
        shrink_late_kernel,
        out_shape=jax.ShapeDtypeStruct((NX, LATE_ROWS, 128), BF16),
        in_specs=[whole()] * 5 + [pl.BlockSpec(memory_space=pl.ANY)],
        out_specs=whole(),
        compiler_params=params(limit=16 * MIB),
        cost_estimate=cost(COST["shrink_late"]),
        name="shrink_late",
    )(far, *guests, *panels, earlier)


def widen(up_ref, owner, wide_up):
    for a in range(LOCAL):
        for c in range(2):
            wide_up[a * 128 + c * 64 : a * 128 + c * 64 + 64, c * 128 : (c + 1) * 128] = up_ref[
                owner * LOCAL + a, c
            ]


def expanded_rows(rows, wide_up, skip, copies):
    which = adapter_of(skip, copies)
    lhs = jnp.concatenate(
        [jnp.where(which == a, rows, jnp.zeros_like(rows)) for a in range(LOCAL)], axis=1
    )
    return jnp.dot(lhs, wide_up[...], preferred_element_type=F32)


def expand_near_kernel(place_ref, mine_ref, other_ref, up_ref, _, *refs):
    outs, wide_up, total, shrunk = refs[:NX], refs[NX], refs[NX + 1], refs[NX + 2]
    z, core = place_ref[1], place_ref[2]
    shrunk[pl.ds(core * 2, 2)] = mine_ref[...]
    shrunk[pl.ds(2 - core * 2, 2)] = other_ref[...]
    wide_up[...] = jnp.zeros_like(wide_up)
    total[...] = jnp.zeros_like(total)
    for k, low, skip in spans(NEAR):
        widen(up_ref, (z + NEAR[k]) & (NZ - 1), wide_up)
        rows = jnp.concatenate([shrunk[e, low : low + WIDE] for e in range(NX)], axis=0)
        y = expanded_rows(rows, wide_up, skip, NX)
        for e in range(NX):
            total[e, low : low + WIDE, :] += y[e * WIDE : (e + 1) * WIDE]
    for e in range(NX):
        outs[e][...] = total[e].astype(BF16)


def expand_near(place, mine, other, up, earlier):
    return pl.pallas_call(
        expand_near_kernel,
        out_shape=[jax.ShapeDtypeStruct((NEAR_ROWS, 256), BF16)] * NX,
        in_specs=[scalars()] + [whole()] * 3 + [pl.BlockSpec(memory_space=pl.ANY)],
        out_specs=[whole()] * NX,
        scratch_shapes=[
            pltpu.VMEM((LOCAL * 128, 256), BF16),
            pltpu.VMEM((NX, NEAR_ROWS, 256), F32),
            pltpu.VMEM((NX, NEAR_ROWS, 128), BF16),
        ],
        compiler_params=params(limit=16 * MIB),
        cost_estimate=cost(COST["expand_near"]),
        name="expand_near",
    )(place, mine, other, up, earlier)


def expand_late_kernel(place_ref, mine_ref, other_ref, up_ref, _, *refs):
    outs, wides, total = refs[:NX], refs[NX : NX + 2], refs[NX + 2]
    z = place_ref[1]
    shrunk = (mine_ref[...].astype(F32) + other_ref[...].astype(F32)).astype(BF16)
    total[...] = jnp.zeros_like(total)
    for k, low, skip in spans(FAR):
        wide_up = wides[k]
        wide_up[...] = jnp.zeros_like(wide_up)
        widen(up_ref, (z + FAR[k]) & (NZ - 1), wide_up)
        rows = jnp.concatenate([shrunk[e, low : low + WIDE] for e in range(NX)], axis=0)
        y = expanded_rows(rows, wide_up, skip, NX)
        for e in range(NX):
            total[e, low : low + WIDE, :] += y[e * WIDE : (e + 1) * WIDE]
    for wide_up, first in ((wides[1], 0), (wides[0], 2)):
        rows = jnp.concatenate([shrunk[first + e, FAR_ROWS:] for e in range(2)], axis=0)
        y = expanded_rows(rows, wide_up, 0, 2)
        for e in range(2):
            total[first + e, FAR_ROWS:, :] = y[e * WIDE : (e + 1) * WIDE]
    for e in range(NX):
        outs[e][...] = total[e].astype(BF16)


def expand_late(place, mine, other, up, earlier):
    return pl.pallas_call(
        expand_late_kernel,
        out_shape=[jax.ShapeDtypeStruct((LATE_ROWS, 256), BF16)] * NX,
        in_specs=[scalars()] + [whole()] * 3 + [pl.BlockSpec(memory_space=pl.ANY)],
        out_specs=[whole()] * NX,
        scratch_shapes=[
            pltpu.VMEM((LOCAL * 128, 256), BF16),
            pltpu.VMEM((LOCAL * 128, 256), BF16),
            pltpu.VMEM((NX, LATE_ROWS, 256), F32),
        ],
        compiler_params=params(limit=16 * MIB),
        cost_estimate=cost(COST["expand_late"]),
        name="expand_late",
    )(place, mine, other, up, earlier)


def gather_kernel(col_ref, base_ref, *refs):
    deltas, out_ref, table = refs[:NX], refs[NX], refs[NX + 1]
    full = table.shape[0]
    filled = NX * NEAR_ROWS

    @pl.when(pl.program_id(0) == 0)
    def _():
        for e in range(NX):
            table[e * NEAR_ROWS : (e + 1) * NEAR_ROWS, :] = deltas[e][...]
        table[filled:, :] = jnp.zeros((full - filled, 256), BF16)

    place = iota((1, full), 1)
    slots = jnp.where(place < filled, place, -1)
    for e in range(1, NX):
        slots = jnp.where(
            (place >= e * NEAR_ROWS) & (place < filled), place + e * LATE_ROWS, slots
        )
    hot = (col_ref[:, :1] == slots).astype(BF16)
    out_ref[...] = base_ref[...].astype(F32) + jnp.dot(
        hot, table[...], preferred_element_type=F32
    )


def gather(col, summed, deltas):
    count = col.shape[0]
    step = 512
    return pl.pallas_call(
        gather_kernel,
        grid=(count // step,),
        out_shape=jax.ShapeDtypeStruct((count, 256), F32),
        in_specs=[
            pl.BlockSpec((step, 128), lambda i: (i, 0)),
            pl.BlockSpec((step, 256), lambda i: (i, 0)),
        ]
        + [pl.BlockSpec(d.shape, lambda i: (0, 0)) for d in deltas],
        out_specs=pl.BlockSpec((step, 256), lambda i: (i, 0)),
        scratch_shapes=[pltpu.VMEM((1536, 256), BF16)],
        compiler_params=params("arbitrary", limit=24 * MIB),
        cost_estimate=cost(COST["gather"]),
        name="gather",
    )(col, summed, *deltas)


def finish_kernel(col_ref, total_ref, *refs):
    deltas, guests, out_ref, both, table = refs[:NX], refs[NX : NX + 2], refs[-3], refs[-2], refs[-1]
    rows, full = col_ref.shape[0], table.shape[0]
    far = NX * FAR_ROWS

    @pl.when(pl.program_id(0) == 0)
    def _():
        for e in range(NX):
            table[e * FAR_ROWS : (e + 1) * FAR_ROWS, :] = deltas[e][:FAR_ROWS, :]
            low = far + e * WIDE
            table[low : low + WIDE, :] = guests[e // 2][e % 2]

    place = iota((1, full), 1)
    slots = place
    for e in range(NX):
        start = e * ROWS + NEAR_ROWS - e * FAR_ROWS
        slots = jnp.where((place >= e * FAR_ROWS) & (place < far), place + start, slots)
        low = far + e * WIDE
        start = e * ROWS + NEAR_ROWS + FAR_ROWS - low
        slots = jnp.where(place >= low, place + start, slots)
    hot = (col_ref[:, :1] == slots).astype(BF16)
    total = total_ref[...] + jnp.dot(hot, table[...], preferred_element_type=F32)
    both[pl.ds(0, rows, stride=2), :] = total[:, :128]
    both[pl.ds(1, rows, stride=2), :] = total[:, 128:]
    out_ref[...] = both[...].astype(BF16)


def finish(col, total, deltas, guests):
    count = col.shape[0]
    step = 512
    return pl.pallas_call(
        finish_kernel,
        grid=(count // step,),
        out_shape=jax.ShapeDtypeStruct((2 * count, 128), BF16),
        in_specs=[
            pl.BlockSpec((step, 128), lambda i: (i, 0)),
            pl.BlockSpec((step, 256), lambda i: (i, 0)),
        ]
        + [pl.BlockSpec(d.shape, lambda i: (0, 0)) for d in deltas]
        + [pl.BlockSpec(g.shape, lambda i: (0, 0, 0)) for g in guests],
        out_specs=pl.BlockSpec((2 * step, 128), lambda i: (i, 0)),
        scratch_shapes=[
            pltpu.VMEM((2 * step, 128), F32),
            pltpu.VMEM((NX * (FAR_ROWS + WIDE), 256), BF16),
        ],
        compiler_params=params("arbitrary", limit=24 * MIB),
        cost_estimate=cost(COST["finish"]),
        name="finish",
    )(col, total, *deltas, *guests)


def along_z(array, d):
    pairs = [(x * NZ + z, x * NZ + (z + d) % NZ) for x in range(NX) for z in range(NZ)]
    return lax.ppermute(array, "ad", pairs)


def along_x(array, d):
    pairs = [(x * NZ + z, (x + d) % NX * NZ + z) for x in range(NX) for z in range(NZ)]
    return lax.ppermute(array, "ad", pairs)


def with_core(array):
    return lax.ppermute(array, "tp", [(i, i ^ 1) for i in range(2 * NY)])


def with_even(array):
    return lax.ppermute(array, "tp", [(i, i ^ 2) for i in range(2 * NY)])


def with_odd(array):
    pairs = [(y * 2 + c, (NY - 1 - y) * 2 + c) for y in range(NY) for c in range(2)]
    return lax.ppermute(array, "tp", pairs)


def add(a, b):
    return (a.astype(F32) + b.astype(F32)).astype(BF16)


def home(deltas):
    return [deltas[0]] + [along_x(deltas[e], -e) for e in (1, 2, 3)]


def body(tokens, weight, down, up, ident, store):
    index, part = lax.axis_index("ad"), lax.axis_index("tp")
    place = jnp.stack([index >> 3, index & 7, part & 1]).astype(I32)
    groups = [[x * NZ + z for z in range(NZ)] for x in range(NX)]

    cw1, ccw1 = along_z(down, 1), along_z(down, -1)
    row, col = route(place, ident.reshape(1, -1), store.reshape(1, -1))
    packed = {e: pack(e, row, tokens) for e in (2, 1, 3)}
    moved = {e: along_x(packed[e], e) for e in (2, 1, 3)}
    xs = [pack(0, row, tokens)] + [moved[e] for e in (1, 2, 3)]
    ups = lax.all_gather(up, "ad", axis_index_groups=groups, tiled=True)

    partial_base = base(tokens, weight, lax.axis_size("tp"), *packed.values())
    cw1, ccw1, partial_base = lax.optimization_barrier((cw1, ccw1, partial_base))
    summed = lax.psum_scatter(partial_base, "tp", scatter_dimension=0, tiled=True)[0]
    cw2, ccw2 = along_z(cw1, 1), along_z(ccw1, -1)
    cw3, ccw3 = along_z(cw2, 1), along_z(ccw2, -1)
    upward, downward = carve(xs)
    guests = [along_z(upward, 1), along_z(downward, -1)]

    keep, send = shrink_near(place, xs, [down, cw1, ccw1, cw2, ccw2], upward)
    near_chip = add(keep, with_core(send))
    near_pair = add(near_chip, with_even(near_chip))
    near = add(near_pair, with_odd(near_pair))
    near = home(expand_near(place, near, with_core(near), ups, near_chip))

    late = shrink_far(xs, [cw3, ccw3], near_chip, ups)
    late = shrink_late(late, guests, [cw3, ccw3], near_pair)
    late = add(late, with_core(late))
    late = add(late, with_even(late))
    total = gather(col, summed, near)
    late = home(expand_late(place, late, with_odd(late), ups, total))
    opposite = [d[FAR_ROWS:] for d in late]
    back = [along_z(jnp.stack(opposite[:2]), -1), along_z(jnp.stack(opposite[2:]), 1)]

    out = finish(col, total, late, back)
    return out.reshape(tokens.shape[0], 2, 128)


def solution(mesh):
    return jax.shard_map(
        body,
        mesh=mesh,
        in_specs=(
            P("ad", "tp"),
            P(None, "tp", None),
            P("ad", "tp", None),
            P("ad", None, None, "tp"),
            P("ad", None),
            P(),
        ),
        out_specs=P("ad", None, "tp"),
        check_vma=False,
    )
```

```python
import functools

import jax
import jax.numpy as jnp
from jax import lax
from jax.experimental import pallas as pl
from jax.experimental.pallas import tpu as pltpu
from jax.sharding import PartitionSpec as P

F32 = jnp.float32
BF16 = jnp.bfloat16
I32 = jnp.int32

NX, NZ = 4, 8
NY = 4
LOCAL = 4
CAP = 18
BLOCK = LOCAL * CAP
WIDE = 80

NEAR = (0, 7, 1, 6, 2)
FAR = (5, 3)
OPPOSITE = 4
NEAR_ROWS = 368
FAR_ROWS = 144
ROWS = 592
LATE_ROWS = ROWS - NEAR_ROWS
START = {offset: k * BLOCK for k, offset in enumerate(NEAR)}
START.update({offset: NEAR_ROWS + k * BLOCK for k, offset in enumerate(FAR)})
START[OPPOSITE] = NEAR_ROWS + FAR_ROWS

MIB = 1024 * 1024
VMEM = 56 * MIB
COST = {
    "route": 3, "pack": 3, "base": 6, "carve": 1, "shrink_near": 3, "expand_near": 3,
    "shrink_far": 100, "shrink_late": 3, "expand_late": 30, "gather": 5, "finish": 5,
}
VMEM = 56 * 1024 * 1024


def iota(shape, dim):
    return lax.broadcasted_iota(I32, shape, dim)


def params(*semantics, limit=VMEM):
    if semantics:
        return pltpu.CompilerParams(vmem_limit_bytes=limit, dimension_semantics=semantics)
    return pltpu.CompilerParams(vmem_limit_bytes=limit)


def cost(micros):
    return pl.CostEstimate(
        flops=int(micros * 1.1e9), bytes_accessed=1000, transcendentals=0
    )


def whole():
    return pl.BlockSpec(memory_space=pltpu.VMEM)


def scalars():
    return pl.BlockSpec(memory_space=pltpu.SMEM)


def route_kernel(place_ref, ids_ref, store_ref, _, row_ref, col_ref):
    x, z = place_ref[0], place_ref[1]
    count = ids_ref.shape[1]
    ids = jnp.broadcast_to(ids_ref[...], (128, count))
    ids_down = ids.T
    store = jnp.broadcast_to(store_ref[...], (128, 128)).T
    for j in range(count // 128):
        mine = ids[:, j * 128 : (j + 1) * 128]
        placed = jnp.sum(
            jnp.where(mine == iota((128, 128), 0), store, 0), axis=0, keepdims=True
        )
        seen = (j + 1) * 128
        same = (ids_down[:seen] == mine[:1]) & (
            iota((seen, 128), 0) < iota((seen, 128), 1) + j * 128
        )
        ordinal = jnp.sum(same.astype(I32), axis=0, keepdims=True)
        owner = placed >> 2
        east = ((owner >> 3) - x) & 3
        north = ((owner & 7) - z) & 7
        start = jnp.zeros_like(owner)
        for offset, first in START.items():
            start = jnp.where(north == offset, first, start)
        row_ref[:, j * 128 : (j + 1) * 128] = (
            east * ROWS + start + (placed & 3) * CAP + ordinal
        )
    col_ref[...] = jnp.broadcast_to(row_ref[...], (128, count)).T


def route(place, ids, store, earlier):
    count = ids.shape[1]
    return pl.pallas_call(
        route_kernel,
        out_shape=(
            jax.ShapeDtypeStruct((1, count), I32),
            jax.ShapeDtypeStruct((count, 128), I32),
        ),
        in_specs=[scalars(), whole(), whole(), pl.BlockSpec(memory_space=pl.ANY)],
        out_specs=(whole(), whole()),
        compiler_params=params(),
        cost_estimate=cost(COST['route']),
        name="route",
    )(place, ids, store, earlier)


def pack_kernel(e, row_ref, tok_ref, out_ref):
    hot = row_ref[...] == iota((ROWS, row_ref.shape[1]), 0) + e * ROWS
    out_ref[...] = jnp.dot(
        hot.astype(BF16), tok_ref[...], preferred_element_type=F32
    ).astype(BF16)


def pack(e, row, tokens):
    return pl.pallas_call(
        functools.partial(pack_kernel, e),
        out_shape=jax.ShapeDtypeStruct((ROWS, tokens.shape[1]), BF16),
        in_specs=[whole()] * 2,
        out_specs=whole(),
        compiler_params=params(limit=24 * MIB),
        cost_estimate=cost(COST["pack"]),
        name="pack",
    )(row, tokens)


def base_kernel(place_ref, tok_ref, w_ref, add_ref, out_ref):
    both = jnp.concatenate([w_ref[0], w_ref[1]], axis=1)
    y = jnp.dot(tok_ref[...], both, preferred_element_type=F32)
    if add_ref is not None:
        y = y + add_ref[0].astype(F32)
    out_ref[0] = y.astype(BF16)


def base(place, tokens, weight, mine, received=None, *earlier):
    count, width = tokens.shape

    def column(i, place_ref):
        core = place_ref[2]
        return (0, 0, i * 2 + (core if mine else 1 - core))

    def kernel(place_ref, tok_ref, w_ref, *refs):
        add_ref = None if received is None else refs[0]
        base_kernel(place_ref, tok_ref, w_ref, add_ref, refs[-1])

    block = pl.BlockSpec((1, count, 256), lambda i, _: (i, 0, 0))
    extra = [] if received is None else [received]
    return pl.pallas_call(
        kernel,
        grid_spec=pltpu.PrefetchScalarGridSpec(
            num_scalar_prefetch=1,
            grid=(NY,),
            in_specs=[
                pl.BlockSpec((count, width), lambda i, _: (0, 0)),
                pl.BlockSpec((2, width, 128), column),
            ]
            + [block] * len(extra)
            + [pl.BlockSpec(memory_space=pl.ANY)] * len(earlier),
            out_specs=block,
        ),
        out_shape=jax.ShapeDtypeStruct((NY, count, 256), BF16),
        compiler_params=params("arbitrary"),
        cost_estimate=cost(COST["base"]),
        name="base",
    )(place, tokens, weight, *extra, *earlier)


def adapter_of(skip, copies):
    row = iota((WIDE, 1), 0) - skip
    which = jnp.full((WIDE, 1), -1, I32)
    for a in range(LOCAL):
        which = jnp.where((row >= a * CAP) & (row < (a + 1) * CAP), a, which)
    return jnp.concatenate([which] * copies, axis=0)


def spans(blocks):
    return [(k, k * BLOCK // 16 * 16, k * BLOCK % 16) for k in range(len(blocks))]


def shrunk_rows(rows, panel, skip, copies):
    y = jnp.dot(
        rows,
        jnp.concatenate([panel[a] for a in range(LOCAL)], axis=1),
        preferred_element_type=F32,
    )
    which = adapter_of(skip, copies)
    kept = jnp.zeros((copies * WIDE, 128), F32)
    for a in range(LOCAL):
        kept = kept + jnp.where(which == a, y[:, a * 128 : (a + 1) * 128], 0.0)
    return kept


def shrink_blocks(xs, panels, blocks, total):
    for k, low, skip in spans(blocks):
        rows = jnp.concatenate([x[low : low + WIDE, :] for x in xs], axis=0)
        kept = shrunk_rows(rows, panels[k], skip, NX)
        for e in range(NX):
            total[e, low : low + WIDE, :] += kept[e * WIDE : (e + 1) * WIDE]


def shrink_near_kernel(place_ref, *refs):
    xs, panels = refs[:NX], refs[NX : NX + len(NEAR)]
    keep_ref, send_ref, total = refs[-3:]
    total[...] = jnp.zeros_like(total)
    shrink_blocks(xs, panels, NEAR, total)
    core = place_ref[2]
    keep_ref[...] = total[pl.ds(core * 2, 2)].astype(BF16)
    send_ref[...] = total[pl.ds(2 - core * 2, 2)].astype(BF16)


def shrink_near(place, xs, panels, *earlier):
    width = xs[0].shape[1]
    half = jax.ShapeDtypeStruct((2, NEAR_ROWS, 128), BF16)
    return pl.pallas_call(
        shrink_near_kernel,
        grid=(1,),
        out_shape=(half, half),
        in_specs=[scalars()]
        + [pl.BlockSpec((pl.Element(NEAR_ROWS), pl.Element(width)), lambda i: (0, 0))] * NX
        + [pl.BlockSpec((LOCAL, width, 128), lambda i: (0, 0, 0)) for w in panels]
        + [pl.BlockSpec(memory_space=pl.ANY)] * len(earlier),
        out_specs=(pl.BlockSpec(half.shape, lambda i: (0, 0, 0)),) * 2,
        scratch_shapes=[pltpu.VMEM((NX, NEAR_ROWS, 128), F32)],
        compiler_params=params("arbitrary"),
        cost_estimate=cost(COST["shrink_near"]),
        name="shrink_near",
    )(place, *xs, *panels, *earlier)


def carve_kernel(*refs):
    xs, outs = refs[:NX], refs[NX:]
    for e in range(NX):
        outs[e // 2][e % 2] = xs[e][...]


def carve(xs):
    width = xs[0].shape[1]
    first = NEAR_ROWS + FAR_ROWS
    pair = jax.ShapeDtypeStruct((2, WIDE, width), BF16)
    return pl.pallas_call(
        carve_kernel,
        grid=(1,),
        out_shape=(pair, pair),
        in_specs=[pl.BlockSpec((pl.Element(WIDE), pl.Element(width)), lambda i: (first, 0))] * NX,
        out_specs=(pl.BlockSpec(pair.shape, lambda i: (0, 0, 0)),) * 2,
        compiler_params=params("arbitrary", limit=8 * MIB),
        cost_estimate=cost(COST["carve"]),
        name="carve",
    )(*xs)


def shrink_far_kernel(*refs):
    xs, panels = refs[:NX], refs[NX : NX + 2]
    out_ref, total = refs[-2:]
    total[...] = jnp.zeros_like(total)
    shrink_blocks(xs, panels, FAR, total)
    out_ref[...] = total[...].astype(BF16)


def shrink_far(xs, panels, *earlier):
    width = xs[0].shape[1]
    return pl.pallas_call(
        shrink_far_kernel,
        grid=(1,),
        out_shape=jax.ShapeDtypeStruct((NX, FAR_ROWS, 128), BF16),
        in_specs=[
            pl.BlockSpec((pl.Element(FAR_ROWS), pl.Element(width)), lambda i: (NEAR_ROWS, 0))
        ]
        * NX
        + [pl.BlockSpec((LOCAL, width, 128), lambda i: (0, 0, 0)) for w in panels]
        + [pl.BlockSpec(memory_space=pl.ANY)] * len(earlier),
        out_specs=pl.BlockSpec((NX, FAR_ROWS, 128), lambda i: (0, 0, 0)),
        scratch_shapes=[pltpu.VMEM((NX, FAR_ROWS, 128), F32)],
        compiler_params=params("arbitrary"),
        cost_estimate=cost(COST["shrink_far"]),
        name="shrink_far",
    )(*xs, *panels, *earlier)


def shrink_late_kernel(far_ref, from_low, from_high, low_ref, high_ref, _, out_ref):
    out_ref[:, :FAR_ROWS, :] = far_ref[...]
    for guest, panel, first in ((from_low, high_ref, 0), (from_high, low_ref, 2)):
        kept = shrunk_rows(jnp.concatenate([guest[0], guest[1]], axis=0), panel, 0, 2)
        for e in range(2):
            out_ref[first + e, FAR_ROWS:, :] = kept[e * WIDE : (e + 1) * WIDE].astype(BF16)


def shrink_late(far, guests, panels, earlier):
    width = guests[0].shape[2]
    return pl.pallas_call(
        shrink_late_kernel,
        grid=(1,),
        out_shape=jax.ShapeDtypeStruct((NX, LATE_ROWS, 128), BF16),
        in_specs=[pl.BlockSpec(a.shape, lambda i: (0, 0, 0)) for a in (far, *guests)]
        + [pl.BlockSpec((LOCAL, width, 128), lambda i: (0, 0, 0)) for w in panels]
        + [pl.BlockSpec(memory_space=pl.ANY)],
        out_specs=pl.BlockSpec((NX, LATE_ROWS, 128), lambda i: (0, 0, 0)),
        compiler_params=params("arbitrary"),
        cost_estimate=cost(COST["shrink_late"]),
        name="shrink_late",
    )(far, *guests, *panels, earlier)


def widen(up_ref, wide_up):
    for a in range(LOCAL):
        for c in range(2):
            wide_up[a * 128 + c * 64 : a * 128 + c * 64 + 64, c * 128 : (c + 1) * 128] = up_ref[
                a, c * 64 : (c + 1) * 64
            ]


def up_block(panel):
    return pl.BlockSpec((LOCAL, 128, 128), lambda i: (0, panel.shape[1] // 128 - 1, 0))


def expanded_rows(rows, wide_up, skip, copies):
    which = adapter_of(skip, copies)
    lhs = jnp.concatenate(
        [jnp.where(which == a, rows, jnp.zeros_like(rows)) for a in range(LOCAL)], axis=1
    )
    return jnp.dot(lhs, wide_up[...], preferred_element_type=F32)


def expand_near_kernel(place_ref, mine_ref, other_ref, *refs):
    ups, outs = refs[: len(NEAR)], refs[len(NEAR) : len(NEAR) + NX]
    wide_up, total, shrunk = refs[len(NEAR) + NX :]
    core = place_ref[2]
    shrunk[pl.ds(core * 2, 2)] = mine_ref[...]
    shrunk[pl.ds(2 - core * 2, 2)] = other_ref[...]
    wide_up[...] = jnp.zeros_like(wide_up)
    total[...] = jnp.zeros_like(total)
    for k, low, skip in spans(NEAR):
        widen(ups[k], wide_up)
        rows = jnp.concatenate([shrunk[e, low : low + WIDE] for e in range(NX)], axis=0)
        y = expanded_rows(rows, wide_up, skip, NX)
        for e in range(NX):
            total[e, low : low + WIDE, :] += y[e * WIDE : (e + 1) * WIDE]
    for e in range(NX):
        outs[e][...] = total[e].astype(BF16)


def expand_near(place, mine, other, panels):
    half = pl.BlockSpec(mine.shape, lambda i: (0, 0, 0))
    return pl.pallas_call(
        expand_near_kernel,
        grid=(1,),
        out_shape=[jax.ShapeDtypeStruct((NEAR_ROWS, 256), BF16)] * NX,
        in_specs=[scalars(), half, half] + [up_block(w) for w in panels],
        out_specs=[pl.BlockSpec((NEAR_ROWS, 256), lambda i: (0, 0))] * NX,
        scratch_shapes=[
            pltpu.VMEM((LOCAL * 128, 256), BF16),
            pltpu.VMEM((NX, NEAR_ROWS, 256), F32),
            pltpu.VMEM((NX, NEAR_ROWS, 128), BF16),
        ],
        compiler_params=params("arbitrary", limit=24 * MIB),
        cost_estimate=cost(COST["expand_near"]),
        name="expand_near",
    )(place, mine, other, *panels)


def expand_late_kernel(mine_ref, other_ref, *refs):
    ups, outs = refs[: len(FAR)], refs[len(FAR) + 1 : len(FAR) + 1 + NX]
    wides, total = refs[-3:-1], refs[-1]
    shrunk = (mine_ref[...].astype(F32) + other_ref[...].astype(F32)).astype(BF16)
    total[...] = jnp.zeros_like(total)
    for k, low, skip in spans(FAR):
        wide_up = wides[k]
        wide_up[...] = jnp.zeros_like(wide_up)
        widen(ups[k], wide_up)
        rows = jnp.concatenate([shrunk[e, low : low + WIDE] for e in range(NX)], axis=0)
        y = expanded_rows(rows, wide_up, skip, NX)
        for e in range(NX):
            total[e, low : low + WIDE, :] += y[e * WIDE : (e + 1) * WIDE]
    for wide_up, first in ((wides[1], 0), (wides[0], 2)):
        rows = jnp.concatenate([shrunk[first + e, FAR_ROWS:] for e in range(2)], axis=0)
        y = expanded_rows(rows, wide_up, 0, 2)
        for e in range(2):
            total[first + e, FAR_ROWS:, :] = y[e * WIDE : (e + 1) * WIDE]
    for e in range(NX):
        outs[e][...] = total[e].astype(BF16)


def expand_late(mine, other, panels, earlier):
    full = pl.BlockSpec(mine.shape, lambda i: (0, 0, 0))
    return pl.pallas_call(
        expand_late_kernel,
        grid=(1,),
        out_shape=[jax.ShapeDtypeStruct((LATE_ROWS, 256), BF16)] * NX,
        in_specs=[full, full]
        + [up_block(w) for w in panels]
        + [pl.BlockSpec(memory_space=pl.ANY)],
        out_specs=[pl.BlockSpec((LATE_ROWS, 256), lambda i: (0, 0))] * NX,
        scratch_shapes=[
            pltpu.VMEM((LOCAL * 128, 256), BF16),
            pltpu.VMEM((LOCAL * 128, 256), BF16),
            pltpu.VMEM((NX, LATE_ROWS, 256), F32),
        ],
        compiler_params=params("arbitrary", limit=24 * MIB),
        cost_estimate=cost(COST["expand_late"]),
        name="expand_late",
    )(mine, other, *panels, earlier)


def gather_kernel(col_ref, base_ref, *refs):
    deltas, out_ref, table = refs[:NX], refs[NX], refs[NX + 1]
    full = table.shape[0]
    filled = NX * NEAR_ROWS

    @pl.when(pl.program_id(0) == 0)
    def _():
        for e in range(NX):
            table[e * NEAR_ROWS : (e + 1) * NEAR_ROWS, :] = deltas[e][...]
        table[filled:, :] = jnp.zeros((full - filled, 256), BF16)

    place = iota((1, full), 1)
    slots = jnp.where(place < filled, place, -1)
    for e in range(1, NX):
        slots = jnp.where(
            (place >= e * NEAR_ROWS) & (place < filled), place + e * LATE_ROWS, slots
        )
    hot = (col_ref[:, :1] == slots).astype(BF16)
    total = jnp.dot(hot, table[...], preferred_element_type=F32)
    for part in range(NY):
        total = total + base_ref[part].astype(F32)
    out_ref[...] = total


def gather(col, parts, deltas):
    count = col.shape[0]
    step = 512
    return pl.pallas_call(
        gather_kernel,
        grid=(count // step,),
        out_shape=jax.ShapeDtypeStruct((count, 256), F32),
        in_specs=[
            pl.BlockSpec((step, 128), lambda i: (i, 0)),
            pl.BlockSpec((NY, step, 256), lambda i: (0, i, 0)),
        ]
        + [pl.BlockSpec(d.shape, lambda i: (0, 0)) for d in deltas],
        out_specs=pl.BlockSpec((step, 256), lambda i: (i, 0)),
        scratch_shapes=[pltpu.VMEM((1536, 256), BF16)],
        compiler_params=params("arbitrary"),
        cost_estimate=cost(COST["gather"]),
        name="gather",
    )(col, parts, *deltas)


def finish_kernel(col_ref, total_ref, *refs):
    deltas, guests, out_ref, both, table = refs[:NX], refs[NX : NX + 2], refs[-3], refs[-2], refs[-1]
    rows, full = col_ref.shape[0], table.shape[0]
    far = NX * FAR_ROWS

    @pl.when(pl.program_id(0) == 0)
    def _():
        for e in range(NX):
            table[e * FAR_ROWS : (e + 1) * FAR_ROWS, :] = deltas[e][:FAR_ROWS, :]
            low = far + e * WIDE
            table[low : low + WIDE, :] = guests[e // 2][e % 2]

    place = iota((1, full), 1)
    slots = place
    for e in range(NX):
        start = e * ROWS + NEAR_ROWS - e * FAR_ROWS
        slots = jnp.where((place >= e * FAR_ROWS) & (place < far), place + start, slots)
        low = far + e * WIDE
        start = e * ROWS + NEAR_ROWS + FAR_ROWS - low
        slots = jnp.where(place >= low, place + start, slots)
    hot = (col_ref[:, :1] == slots).astype(BF16)
    total = total_ref[...] + jnp.dot(hot, table[...], preferred_element_type=F32)
    both[pl.ds(0, rows, stride=2), :] = total[:, :128]
    both[pl.ds(1, rows, stride=2), :] = total[:, 128:]
    out_ref[...] = both[...].astype(BF16)


def finish(col, total, deltas, guests):
    count = col.shape[0]
    step = 512
    return pl.pallas_call(
        finish_kernel,
        grid=(count // step,),
        out_shape=jax.ShapeDtypeStruct((2 * count, 128), BF16),
        in_specs=[
            pl.BlockSpec((step, 128), lambda i: (i, 0)),
            pl.BlockSpec((step, 256), lambda i: (i, 0)),
        ]
        + [pl.BlockSpec(d.shape, lambda i: (0, 0)) for d in deltas]
        + [pl.BlockSpec(g.shape, lambda i: (0, 0, 0)) for g in guests],
        out_specs=pl.BlockSpec((2 * step, 128), lambda i: (i, 0)),
        scratch_shapes=[
            pltpu.VMEM((2 * step, 128), F32),
            pltpu.VMEM((NX * (FAR_ROWS + WIDE), 256), BF16),
        ],
        compiler_params=params("arbitrary", limit=24 * MIB),
        cost_estimate=cost(COST["finish"]),
        name="finish",
    )(col, total, *deltas, *guests)


def along_z(array, d):
    pairs = [(x * NZ + z, x * NZ + (z + d) % NZ) for x in range(NX) for z in range(NZ)]
    return lax.ppermute(array, "ad", pairs)


def along_x(array, d):
    pairs = [(x * NZ + z, (x + d) % NX * NZ + z) for x in range(NX) for z in range(NZ)]
    return lax.ppermute(array, "ad", pairs)


def with_core(array):
    return lax.ppermute(array, "tp", [(i, i ^ 1) for i in range(2 * NY)])


def with_even(array):
    return lax.ppermute(array, "tp", [(i, i ^ 2) for i in range(2 * NY)])


def with_odd(array):
    pairs = [(y * 2 + c, (NY - 1 - y) * 2 + c) for y in range(NY) for c in range(2)]
    return lax.ppermute(array, "tp", pairs)


def add(a, b):
    return (a.astype(F32) + b.astype(F32)).astype(BF16)


def home(deltas):
    return [deltas[0]] + [along_x(deltas[e], -e) for e in (1, 2, 3)]


def body(tokens, weight, down, up, ident, store):
    index, part = lax.axis_index("ad"), lax.axis_index("tp")
    place = jnp.stack([index >> 3, index & 7, part & 1]).astype(I32)
    columns = [[y * 2 + c for y in range(NY)] for c in range(2)]

    panels = jnp.concatenate([down, up.reshape(LOCAL, 128, 128)], axis=1)
    cw1, ccw1 = along_z(panels, 1), along_z(panels, -1)

    sent = base(place, tokens, weight, False)
    received = with_core(sent)
    row, col = route(place, ident.reshape(1, -1), store.reshape(1, -1), sent)
    packed = {e: pack(e, row, tokens) for e in (2, 1, 3)}
    moved = {e: along_x(packed[e], e) for e in (2, 1, 3)}
    xs = [pack(0, row, tokens)] + [moved[e] for e in (1, 2, 3)]
    chip_base = base(place, tokens, weight, True, received, *packed.values())
    cw1, ccw1, chip_base = lax.optimization_barrier((cw1, ccw1, chip_base))
    parts = lax.all_to_all(chip_base, "tp", 0, 0, axis_index_groups=columns, tiled=True)

    cw2, ccw2 = along_z(cw1, 1), along_z(ccw1, -1)
    cw3, ccw3 = along_z(cw2, 1), along_z(ccw2, -1)
    upward, downward = carve(xs)
    guests = [along_z(upward, 1), along_z(downward, -1)]

    held = [panels, cw1, ccw1, cw2, ccw2]
    keep, send = shrink_near(place, xs, held, upward)
    near_chip = add(keep, with_core(send))
    near_pair = add(near_chip, with_even(near_chip))
    near = add(near_pair, with_odd(near_pair))
    near = home(expand_near(place, near, with_core(near), held))

    late = shrink_far(xs, [cw3, ccw3], near_chip, parts)
    late = shrink_late(late, guests, [cw3, ccw3], near_pair)
    late = add(late, with_core(late))
    late = add(late, with_even(late))
    total = gather(col, parts, near)
    late = home(expand_late(late, with_odd(late), [cw3, ccw3], total))
    opposite = [d[FAR_ROWS:] for d in late]
    back = [along_z(jnp.stack(opposite[:2]), -1), along_z(jnp.stack(opposite[2:]), 1)]

    out = finish(col, total, late, back)
    return out.reshape(tokens.shape[0], 2, 128)


def solution(mesh):
    return jax.shard_map(
        body,
        mesh=mesh,
        in_specs=(
            P("ad", "tp"),
            P(None, "tp", None),
            P("ad", "tp", None),
            P("ad", None, None, "tp"),
            P("ad", None),
            P(),
        ),
        out_specs=P("ad", None, "tp"),
        check_vma=False,
    )
```

```python
import functools

import jax
import jax.numpy as jnp
from jax import lax
from jax.experimental import pallas as pl
from jax.experimental.pallas import tpu as pltpu
from jax.sharding import PartitionSpec as P

F32 = jnp.float32
BF16 = jnp.bfloat16
I32 = jnp.int32

NX, NZ = 4, 8
NY = 4
LOCAL = 4
CAP = 18
BLOCK = LOCAL * CAP
WIDE = 80

NEAR = (0, 7, 1, 6, 2)
FAR = (5, 3)
OPPOSITE = 4
NEAR_ROWS = 368
FAR_ROWS = 144
ROWS = 592
LATE_ROWS = ROWS - NEAR_ROWS
START = {offset: k * BLOCK for k, offset in enumerate(NEAR)}
START.update({offset: NEAR_ROWS + k * BLOCK for k, offset in enumerate(FAR)})
START[OPPOSITE] = NEAR_ROWS + FAR_ROWS

MIB = 1024 * 1024
VMEM = 56 * MIB
COST = {
    "route": 3, "pack": 3, "columns": 2, "base": 11, "carve": 1, "shrink_near": 3, "expand_near": 3,
    "shrink_far": 100, "shrink_late": 3, "expand_late": 30, "gather": 5, "finish": 5,
}
VMEM = 56 * 1024 * 1024


def iota(shape, dim):
    return lax.broadcasted_iota(I32, shape, dim)


def params(*semantics, limit=VMEM):
    if semantics:
        return pltpu.CompilerParams(vmem_limit_bytes=limit, dimension_semantics=semantics)
    return pltpu.CompilerParams(vmem_limit_bytes=limit)


def cost(micros):
    return pl.CostEstimate(
        flops=int(micros * 1.1e9), bytes_accessed=1000, transcendentals=0
    )


def whole():
    return pl.BlockSpec(memory_space=pltpu.VMEM)


def scalars():
    return pl.BlockSpec(memory_space=pltpu.SMEM)


def route_kernel(place_ref, ids_ref, store_ref, row_ref, col_ref):
    x, z = place_ref[0], place_ref[1]
    count = ids_ref.shape[1]
    ids = jnp.broadcast_to(ids_ref[...], (128, count))
    ids_down = ids.T
    store = jnp.broadcast_to(store_ref[...], (128, 128)).T
    for j in range(count // 128):
        mine = ids[:, j * 128 : (j + 1) * 128]
        placed = jnp.sum(
            jnp.where(mine == iota((128, 128), 0), store, 0), axis=0, keepdims=True
        )
        seen = (j + 1) * 128
        same = (ids_down[:seen] == mine[:1]) & (
            iota((seen, 128), 0) < iota((seen, 128), 1) + j * 128
        )
        ordinal = jnp.sum(same.astype(I32), axis=0, keepdims=True)
        owner = placed >> 2
        east = ((owner >> 3) - x) & 3
        north = ((owner & 7) - z) & 7
        start = jnp.zeros_like(owner)
        for offset, first in START.items():
            start = jnp.where(north == offset, first, start)
        row_ref[:, j * 128 : (j + 1) * 128] = (
            east * ROWS + start + (placed & 3) * CAP + ordinal
        )
    col_ref[...] = jnp.broadcast_to(row_ref[...], (128, count)).T


def route(place, ids, store):
    count = ids.shape[1]
    return pl.pallas_call(
        route_kernel,
        out_shape=(
            jax.ShapeDtypeStruct((1, count), I32),
            jax.ShapeDtypeStruct((count, 128), I32),
        ),
        in_specs=[scalars(), whole(), whole()],
        out_specs=(whole(), whole()),
        compiler_params=params(),
        cost_estimate=cost(COST['route']),
        name="route",
    )(place, ids, store)


def pack_kernel(e, row_ref, tok_ref, *refs):
    out_ref = refs[-1]
    hot = row_ref[...] == iota((ROWS, row_ref.shape[1]), 0) + e * ROWS
    out_ref[...] = jnp.dot(
        hot.astype(BF16), tok_ref[...], preferred_element_type=F32
    ).astype(BF16)


def pack(e, row, tokens, *earlier):
    return pl.pallas_call(
        functools.partial(pack_kernel, e),
        out_shape=jax.ShapeDtypeStruct((ROWS, tokens.shape[1]), BF16),
        in_specs=[whole()] * 2 + [pl.BlockSpec(memory_space=pl.ANY)] * len(earlier),
        out_specs=whole(),
        compiler_params=params(limit=24 * MIB),
        cost_estimate=cost(COST["pack"]),
        name="pack",
    )(row, tokens, *earlier)


def columns_kernel(place_ref, w_ref, out_ref):
    out_ref[...] = w_ref[...]


def other_columns(place, weight):
    width = weight.shape[1]
    return pl.pallas_call(
        columns_kernel,
        grid_spec=pltpu.PrefetchScalarGridSpec(
            num_scalar_prefetch=1,
            grid=(NY,),
            in_specs=[
                pl.BlockSpec((2, width, 128), lambda i, place: (0, 0, i * 2 + 1 - place[2]))
            ],
            out_specs=pl.BlockSpec((2, width, 128), lambda i, place: (0, 0, i)),
        ),
        out_shape=jax.ShapeDtypeStruct((2, width, NY * 128), BF16),
        compiler_params=params("arbitrary"),
        cost_estimate=cost(COST["columns"]),
        name="columns",
    )(place, weight)


def base_kernel(place_ref, tok_ref, w_ref, other_tok_ref, other_w_ref, *refs):
    total = jnp.zeros(refs[-1].shape[1:], F32)
    for t_ref, panel_ref in ((tok_ref, w_ref), (other_tok_ref, other_w_ref)):
        both = jnp.concatenate([panel_ref[0], panel_ref[1]], axis=1)
        total = total + jnp.dot(t_ref[...], both, preferred_element_type=F32)
    refs[-1][0] = total.astype(BF16)


def base(place, tokens, weight, other_tokens, other_weight, *earlier):
    count, width = tokens.shape
    rows = pl.BlockSpec((count, width), lambda i, place: (0, 0))
    return pl.pallas_call(
        base_kernel,
        grid_spec=pltpu.PrefetchScalarGridSpec(
            num_scalar_prefetch=1,
            grid=(NY,),
            in_specs=[
                rows,
                pl.BlockSpec((2, width, 128), lambda i, place: (0, 0, i * 2 + place[2])),
                rows,
                pl.BlockSpec((2, width, 128), lambda i, place: (0, 0, i)),
            ]
            + [pl.BlockSpec(memory_space=pl.ANY)] * len(earlier),
            out_specs=pl.BlockSpec((1, count, 256), lambda i, place: (i, 0, 0)),
        ),
        out_shape=jax.ShapeDtypeStruct((NY, count, 256), BF16),
        compiler_params=params("arbitrary"),
        cost_estimate=cost(COST["base"]),
        name="base",
    )(place, tokens, weight, other_tokens, other_weight, *earlier)


def adapter_of(skip, copies):
    row = iota((WIDE, 1), 0) - skip
    which = jnp.full((WIDE, 1), -1, I32)
    for a in range(LOCAL):
        which = jnp.where((row >= a * CAP) & (row < (a + 1) * CAP), a, which)
    return jnp.concatenate([which] * copies, axis=0)


def spans(blocks):
    return [(k, k * BLOCK // 16 * 16, k * BLOCK % 16) for k in range(len(blocks))]


def shrunk_rows(rows, panel, skip, copies):
    y = jnp.dot(
        rows,
        jnp.concatenate([panel[a] for a in range(LOCAL)], axis=1),
        preferred_element_type=F32,
    )
    which = adapter_of(skip, copies)
    kept = jnp.zeros((copies * WIDE, 128), F32)
    for a in range(LOCAL):
        kept = kept + jnp.where(which == a, y[:, a * 128 : (a + 1) * 128], 0.0)
    return kept


def shrink_blocks(xs, panels, blocks, total):
    for k, low, skip in spans(blocks):
        rows = jnp.concatenate([x[low : low + WIDE, :] for x in xs], axis=0)
        kept = shrunk_rows(rows, panels[k], skip, NX)
        for e in range(NX):
            total[e, low : low + WIDE, :] += kept[e * WIDE : (e + 1) * WIDE]


def shrink_near_kernel(place_ref, *refs):
    xs, panels = refs[:NX], refs[NX : NX + len(NEAR)]
    keep_ref, send_ref, total = refs[-3:]
    total[...] = jnp.zeros_like(total)
    shrink_blocks(xs, panels, NEAR, total)
    core = place_ref[2]
    keep_ref[...] = total[pl.ds(core * 2, 2)].astype(BF16)
    send_ref[...] = total[pl.ds(2 - core * 2, 2)].astype(BF16)


def shrink_near(place, xs, panels, *earlier):
    width = xs[0].shape[1]
    half = jax.ShapeDtypeStruct((2, NEAR_ROWS, 128), BF16)
    return pl.pallas_call(
        shrink_near_kernel,
        grid=(1,),
        out_shape=(half, half),
        in_specs=[scalars()]
        + [pl.BlockSpec((pl.Element(NEAR_ROWS), pl.Element(width)), lambda i: (0, 0))] * NX
        + [pl.BlockSpec((LOCAL, width, 128), lambda i: (0, 0, 0)) for w in panels]
        + [pl.BlockSpec(memory_space=pl.ANY)] * len(earlier),
        out_specs=(pl.BlockSpec(half.shape, lambda i: (0, 0, 0)),) * 2,
        scratch_shapes=[pltpu.VMEM((NX, NEAR_ROWS, 128), F32)],
        compiler_params=params("arbitrary", limit=32 * MIB),
        cost_estimate=cost(COST["shrink_near"]),
        name="shrink_near",
    )(place, *xs, *panels, *earlier)


def carve_kernel(*refs):
    xs, outs = refs[:NX], refs[NX:]
    for e in range(NX):
        outs[e // 2][e % 2] = xs[e][...]


def carve(xs):
    width = xs[0].shape[1]
    first = NEAR_ROWS + FAR_ROWS
    pair = jax.ShapeDtypeStruct((2, WIDE, width), BF16)
    return pl.pallas_call(
        carve_kernel,
        grid=(1,),
        out_shape=(pair, pair),
        in_specs=[pl.BlockSpec((pl.Element(WIDE), pl.Element(width)), lambda i: (first, 0))] * NX,
        out_specs=(pl.BlockSpec(pair.shape, lambda i: (0, 0, 0)),) * 2,
        compiler_params=params("arbitrary", limit=8 * MIB),
        cost_estimate=cost(COST["carve"]),
        name="carve",
    )(*xs)


def shrink_far_kernel(*refs):
    xs, panels = refs[:NX], refs[NX : NX + 2]
    out_ref, total = refs[-2:]
    total[...] = jnp.zeros_like(total)
    shrink_blocks(xs, panels, FAR, total)
    out_ref[...] = total[...].astype(BF16)


def shrink_far(xs, panels, *earlier):
    width = xs[0].shape[1]
    return pl.pallas_call(
        shrink_far_kernel,
        grid=(1,),
        out_shape=jax.ShapeDtypeStruct((NX, FAR_ROWS, 128), BF16),
        in_specs=[
            pl.BlockSpec((pl.Element(FAR_ROWS), pl.Element(width)), lambda i: (NEAR_ROWS, 0))
        ]
        * NX
        + [pl.BlockSpec((LOCAL, width, 128), lambda i: (0, 0, 0)) for w in panels]
        + [pl.BlockSpec(memory_space=pl.ANY)] * len(earlier),
        out_specs=pl.BlockSpec((NX, FAR_ROWS, 128), lambda i: (0, 0, 0)),
        scratch_shapes=[pltpu.VMEM((NX, FAR_ROWS, 128), F32)],
        compiler_params=params("arbitrary", limit=16 * MIB),
        cost_estimate=cost(COST["shrink_far"]),
        name="shrink_far",
    )(*xs, *panels, *earlier)


def shrink_late_kernel(far_ref, from_low, from_high, low_ref, high_ref, _, out_ref):
    out_ref[:, :FAR_ROWS, :] = far_ref[...]
    for guest, panel, first in ((from_low, high_ref, 0), (from_high, low_ref, 2)):
        kept = shrunk_rows(jnp.concatenate([guest[0], guest[1]], axis=0), panel, 0, 2)
        for e in range(2):
            out_ref[first + e, FAR_ROWS:, :] = kept[e * WIDE : (e + 1) * WIDE].astype(BF16)


def shrink_late(far, guests, panels, earlier):
    width = guests[0].shape[2]
    return pl.pallas_call(
        shrink_late_kernel,
        grid=(1,),
        out_shape=jax.ShapeDtypeStruct((NX, LATE_ROWS, 128), BF16),
        in_specs=[pl.BlockSpec(a.shape, lambda i: (0, 0, 0)) for a in (far, *guests)]
        + [pl.BlockSpec((LOCAL, width, 128), lambda i: (0, 0, 0)) for w in panels]
        + [pl.BlockSpec(memory_space=pl.ANY)],
        out_specs=pl.BlockSpec((NX, LATE_ROWS, 128), lambda i: (0, 0, 0)),
        compiler_params=params("arbitrary", limit=16 * MIB),
        cost_estimate=cost(COST["shrink_late"]),
        name="shrink_late",
    )(far, *guests, *panels, earlier)


def widen(up_ref, wide_up):
    for a in range(LOCAL):
        for c in range(2):
            wide_up[a * 128 + c * 64 : a * 128 + c * 64 + 64, c * 128 : (c + 1) * 128] = up_ref[
                a, c * 64 : (c + 1) * 64
            ]


def up_block(panel):
    return pl.BlockSpec((LOCAL, 128, 128), lambda i: (0, panel.shape[1] // 128 - 1, 0))


def expanded_rows(rows, wide_up, skip, copies):
    which = adapter_of(skip, copies)
    lhs = jnp.concatenate(
        [jnp.where(which == a, rows, jnp.zeros_like(rows)) for a in range(LOCAL)], axis=1
    )
    return jnp.dot(lhs, wide_up[...], preferred_element_type=F32)


def expand_near_kernel(place_ref, mine_ref, other_ref, *refs):
    ups, outs = refs[: len(NEAR)], refs[len(NEAR) : len(NEAR) + NX]
    wide_up, total, shrunk = refs[len(NEAR) + NX :]
    core = place_ref[2]
    shrunk[pl.ds(core * 2, 2)] = mine_ref[...]
    shrunk[pl.ds(2 - core * 2, 2)] = other_ref[...]
    wide_up[...] = jnp.zeros_like(wide_up)
    total[...] = jnp.zeros_like(total)
    for k, low, skip in spans(NEAR):
        widen(ups[k], wide_up)
        rows = jnp.concatenate([shrunk[e, low : low + WIDE] for e in range(NX)], axis=0)
        y = expanded_rows(rows, wide_up, skip, NX)
        for e in range(NX):
            total[e, low : low + WIDE, :] += y[e * WIDE : (e + 1) * WIDE]
    for e in range(NX):
        outs[e][...] = total[e].astype(BF16)


def expand_near(place, mine, other, panels):
    half = pl.BlockSpec(mine.shape, lambda i: (0, 0, 0))
    return pl.pallas_call(
        expand_near_kernel,
        grid=(1,),
        out_shape=[jax.ShapeDtypeStruct((NEAR_ROWS, 256), BF16)] * NX,
        in_specs=[scalars(), half, half] + [up_block(w) for w in panels],
        out_specs=[pl.BlockSpec((NEAR_ROWS, 256), lambda i: (0, 0))] * NX,
        scratch_shapes=[
            pltpu.VMEM((LOCAL * 128, 256), BF16),
            pltpu.VMEM((NX, NEAR_ROWS, 256), F32),
            pltpu.VMEM((NX, NEAR_ROWS, 128), BF16),
        ],
        compiler_params=params("arbitrary", limit=24 * MIB),
        cost_estimate=cost(COST["expand_near"]),
        name="expand_near",
    )(place, mine, other, *panels)


def expand_late_kernel(mine_ref, other_ref, *refs):
    ups, outs = refs[: len(FAR)], refs[-3 - NX : -3]
    wides, total = refs[-3:-1], refs[-1]
    shrunk = (mine_ref[...].astype(F32) + other_ref[...].astype(F32)).astype(BF16)
    total[...] = jnp.zeros_like(total)
    for k, low, skip in spans(FAR):
        wide_up = wides[k]
        wide_up[...] = jnp.zeros_like(wide_up)
        widen(ups[k], wide_up)
        rows = jnp.concatenate([shrunk[e, low : low + WIDE] for e in range(NX)], axis=0)
        y = expanded_rows(rows, wide_up, skip, NX)
        for e in range(NX):
            total[e, low : low + WIDE, :] += y[e * WIDE : (e + 1) * WIDE]
    for wide_up, first in ((wides[1], 0), (wides[0], 2)):
        rows = jnp.concatenate([shrunk[first + e, FAR_ROWS:] for e in range(2)], axis=0)
        y = expanded_rows(rows, wide_up, 0, 2)
        for e in range(2):
            total[first + e, FAR_ROWS:, :] = y[e * WIDE : (e + 1) * WIDE]
    for e in range(NX):
        outs[e][...] = total[e].astype(BF16)


def expand_late(mine, other, panels, *earlier):
    full = pl.BlockSpec(mine.shape, lambda i: (0, 0, 0))
    return pl.pallas_call(
        expand_late_kernel,
        grid=(1,),
        out_shape=[jax.ShapeDtypeStruct((LATE_ROWS, 256), BF16)] * NX,
        in_specs=[full, full]
        + [up_block(w) for w in panels]
        + [pl.BlockSpec(memory_space=pl.ANY)] * len(earlier),
        out_specs=[pl.BlockSpec((LATE_ROWS, 256), lambda i: (0, 0))] * NX,
        scratch_shapes=[
            pltpu.VMEM((LOCAL * 128, 256), BF16),
            pltpu.VMEM((LOCAL * 128, 256), BF16),
            pltpu.VMEM((NX, LATE_ROWS, 256), F32),
        ],
        compiler_params=params("arbitrary", limit=24 * MIB),
        cost_estimate=cost(COST["expand_late"]),
        name="expand_late",
    )(mine, other, *panels, *earlier)


def gather_kernel(col_ref, base_ref, *refs):
    deltas, out_ref, table = refs[:NX], refs[NX], refs[NX + 1]
    full = table.shape[0]
    filled = NX * NEAR_ROWS

    @pl.when(pl.program_id(0) == 0)
    def _():
        for e in range(NX):
            table[e * NEAR_ROWS : (e + 1) * NEAR_ROWS, :] = deltas[e][...]
        table[filled:, :] = jnp.zeros((full - filled, 256), BF16)

    place = iota((1, full), 1)
    slots = jnp.where(place < filled, place, -1)
    for e in range(1, NX):
        slots = jnp.where(
            (place >= e * NEAR_ROWS) & (place < filled), place + e * LATE_ROWS, slots
        )
    hot = (col_ref[:, :1] == slots).astype(BF16)
    total = jnp.dot(hot, table[...], preferred_element_type=F32)
    for part in range(NY):
        total = total + base_ref[part].astype(F32)
    out_ref[...] = total


def gather(col, parts, deltas):
    count = col.shape[0]
    step = 512
    return pl.pallas_call(
        gather_kernel,
        grid=(count // step,),
        out_shape=jax.ShapeDtypeStruct((count, 256), F32),
        in_specs=[
            pl.BlockSpec((step, 128), lambda i: (i, 0)),
            pl.BlockSpec((NY, step, 256), lambda i: (0, i, 0)),
        ]
        + [pl.BlockSpec(d.shape, lambda i: (0, 0)) for d in deltas],
        out_specs=pl.BlockSpec((step, 256), lambda i: (i, 0)),
        scratch_shapes=[pltpu.VMEM((1536, 256), BF16)],
        compiler_params=params("arbitrary"),
        cost_estimate=cost(COST["gather"]),
        name="gather",
    )(col, parts, *deltas)


def finish_kernel(col_ref, total_ref, *refs):
    deltas, guests, out_ref, both, table = refs[:NX], refs[NX : NX + 2], refs[-3], refs[-2], refs[-1]
    rows, full = col_ref.shape[0], table.shape[0]
    far = NX * FAR_ROWS

    @pl.when(pl.program_id(0) == 0)
    def _():
        for e in range(NX):
            table[e * FAR_ROWS : (e + 1) * FAR_ROWS, :] = deltas[e][:FAR_ROWS, :]
            low = far + e * WIDE
            table[low : low + WIDE, :] = guests[e // 2][e % 2]

    place = iota((1, full), 1)
    slots = place
    for e in range(NX):
        start = e * ROWS + NEAR_ROWS - e * FAR_ROWS
        slots = jnp.where((place >= e * FAR_ROWS) & (place < far), place + start, slots)
        low = far + e * WIDE
        start = e * ROWS + NEAR_ROWS + FAR_ROWS - low
        slots = jnp.where(place >= low, place + start, slots)
    hot = (col_ref[:, :1] == slots).astype(BF16)
    total = total_ref[...] + jnp.dot(hot, table[...], preferred_element_type=F32)
    both[pl.ds(0, rows, stride=2), :] = total[:, :128]
    both[pl.ds(1, rows, stride=2), :] = total[:, 128:]
    out_ref[...] = both[...].astype(BF16)


def finish(col, total, deltas, guests):
    count = col.shape[0]
    step = 512
    return pl.pallas_call(
        finish_kernel,
        grid=(count // step,),
        out_shape=jax.ShapeDtypeStruct((2 * count, 128), BF16),
        in_specs=[
            pl.BlockSpec((step, 128), lambda i: (i, 0)),
            pl.BlockSpec((step, 256), lambda i: (i, 0)),
        ]
        + [pl.BlockSpec(d.shape, lambda i: (0, 0)) for d in deltas]
        + [pl.BlockSpec(g.shape, lambda i: (0, 0, 0)) for g in guests],
        out_specs=pl.BlockSpec((2 * step, 128), lambda i: (i, 0)),
        scratch_shapes=[
            pltpu.VMEM((2 * step, 128), F32),
            pltpu.VMEM((NX * (FAR_ROWS + WIDE), 256), BF16),
        ],
        compiler_params=params("arbitrary", limit=24 * MIB),
        cost_estimate=cost(COST["finish"]),
        name="finish",
    )(col, total, *deltas, *guests)


def along_z(array, d):
    pairs = [(x * NZ + z, x * NZ + (z + d) % NZ) for x in range(NX) for z in range(NZ)]
    return lax.ppermute(array, "ad", pairs)


def along_x(array, d):
    pairs = [(x * NZ + z, (x + d) % NX * NZ + z) for x in range(NX) for z in range(NZ)]
    return lax.ppermute(array, "ad", pairs)


def with_core(array):
    return lax.ppermute(array, "tp", [(i, i ^ 1) for i in range(2 * NY)])


def with_even(array):
    return lax.ppermute(array, "tp", [(i, i ^ 2) for i in range(2 * NY)])


def with_odd(array):
    pairs = [(y * 2 + c, (NY - 1 - y) * 2 + c) for y in range(NY) for c in range(2)]
    return lax.ppermute(array, "tp", pairs)


def add(a, b):
    return (a.astype(F32) + b.astype(F32)).astype(BF16)


def home(deltas):
    return [deltas[0]] + [along_x(deltas[e], -e) for e in (1, 2, 3)]


def body(tokens, weight, down, up, ident, store):
    index, part = lax.axis_index("ad"), lax.axis_index("tp")
    place = jnp.stack([index >> 3, index & 7, part & 1]).astype(I32)
    columns = [[y * 2 + c for y in range(NY)] for c in range(2)]

    panels = jnp.concatenate([down, up.reshape(LOCAL, 128, 128)], axis=1)
    cw1, ccw1 = along_z(panels, 1), along_z(panels, -1)

    other_tokens = with_core(tokens)
    other_weight = with_core(other_columns(place, weight))
    row, col = route(place, ident.reshape(1, -1), store.reshape(1, -1))
    packed = {e: pack(e, row, tokens) for e in (1, 3, 2)}
    moved = {e: along_x(packed[e], e) for e in (1, 3, 2)}
    xs = [pack(0, row, tokens)] + [moved[e] for e in (1, 2, 3)]
    chip_base = base(place, tokens, weight, other_tokens, other_weight, *packed.values())
    cw1, ccw1, chip_base = lax.optimization_barrier((cw1, ccw1, chip_base))
    parts = lax.all_to_all(chip_base, "tp", 0, 0, axis_index_groups=columns, tiled=True)

    cw2, ccw2 = along_z(cw1, 1), along_z(ccw1, -1)
    cw3, ccw3 = along_z(cw2, 1), along_z(ccw2, -1)
    upward, downward = carve(xs)
    guests = [along_z(upward, 1), along_z(downward, -1)]

    held = [panels, cw1, ccw1, cw2, ccw2]
    keep, send = shrink_near(place, xs, held, upward)
    near_chip = add(keep, with_core(send))
    near_pair = add(near_chip, with_even(near_chip))
    near = add(near_pair, with_odd(near_pair))
    near = home(expand_near(place, near, with_core(near), held))

    late = shrink_far(xs, [cw3, ccw3], near_chip, parts)
    late = shrink_late(late, guests, [cw3, ccw3], near_pair)
    late = add(late, with_core(late))
    late = add(late, with_even(late))
    total = gather(col, parts, near)
    late = home(expand_late(late, with_odd(late), [cw3, ccw3], *near[1:]))
    opposite = [d[FAR_ROWS:] for d in late]
    back = [along_z(jnp.stack(opposite[:2]), -1), along_z(jnp.stack(opposite[2:]), 1)]

    out = finish(col, total, late, back)
    return out.reshape(tokens.shape[0], 2, 128)


def solution(mesh):
    return jax.shard_map(
        body,
        mesh=mesh,
        in_specs=(
            P("ad", "tp"),
            P(None, "tp", None),
            P("ad", "tp", None),
            P("ad", None, None, "tp"),
            P("ad", None),
            P(),
        ),
        out_specs=P("ad", None, "tp"),
        check_vma=False,
    )
```

```python
import functools

import jax
import jax.numpy as jnp
from jax import lax
from jax.experimental import pallas as pl
from jax.experimental.pallas import tpu as pltpu
from jax.sharding import PartitionSpec as P

F32 = jnp.float32
BF16 = jnp.bfloat16
I32 = jnp.int32

NX, NZ = 4, 8
NY = 4
LOCAL = 4
CAP = 18
BLOCK = LOCAL * CAP
WIDE = 80

NEAR = (0, 7, 1, 6, 2)
FAR = (5, 3)
OPPOSITE = 4
NEAR_ROWS = 368
FAR_ROWS = 144
ROWS = 592
LATE_ROWS = ROWS - NEAR_ROWS
START = {offset: k * BLOCK for k, offset in enumerate(NEAR)}
START.update({offset: NEAR_ROWS + k * BLOCK for k, offset in enumerate(FAR)})
START[OPPOSITE] = NEAR_ROWS + FAR_ROWS

MIB = 1024 * 1024
VMEM = 56 * MIB
COST = {
    "route": 3, "pack": 3, "base": 11, "carve": 1, "shrink_near": 3, "expand_near": 3,
    "shrink_far": 100, "shrink_late": 3, "expand_late": 30, "gather": 5, "finish": 5,
}
VMEM = 56 * 1024 * 1024


def iota(shape, dim):
    return lax.broadcasted_iota(I32, shape, dim)


def params(*semantics, limit=VMEM):
    if semantics:
        return pltpu.CompilerParams(vmem_limit_bytes=limit, dimension_semantics=semantics)
    return pltpu.CompilerParams(vmem_limit_bytes=limit)


def cost(micros):
    return pl.CostEstimate(
        flops=int(micros * 1.1e9), bytes_accessed=1000, transcendentals=0
    )


def whole():
    return pl.BlockSpec(memory_space=pltpu.VMEM)


def scalars():
    return pl.BlockSpec(memory_space=pltpu.SMEM)


def route_kernel(place_ref, ids_ref, store_ref, row_ref, col_ref):
    x, z = place_ref[0], place_ref[1]
    count = ids_ref.shape[1]
    ids = jnp.broadcast_to(ids_ref[...], (128, count))
    ids_down = ids.T
    store = jnp.broadcast_to(store_ref[...], (128, 128)).T
    for j in range(count // 128):
        mine = ids[:, j * 128 : (j + 1) * 128]
        placed = jnp.sum(
            jnp.where(mine == iota((128, 128), 0), store, 0), axis=0, keepdims=True
        )
        seen = (j + 1) * 128
        same = (ids_down[:seen] == mine[:1]) & (
            iota((seen, 128), 0) < iota((seen, 128), 1) + j * 128
        )
        ordinal = jnp.sum(same.astype(I32), axis=0, keepdims=True)
        owner = placed >> 2
        east = ((owner >> 3) - x) & 3
        north = ((owner & 7) - z) & 7
        start = jnp.zeros_like(owner)
        for offset, first in START.items():
            start = jnp.where(north == offset, first, start)
        row_ref[:, j * 128 : (j + 1) * 128] = (
            east * ROWS + start + (placed & 3) * CAP + ordinal
        )
    col_ref[...] = jnp.broadcast_to(row_ref[...], (128, count)).T


def route(place, ids, store):
    count = ids.shape[1]
    return pl.pallas_call(
        route_kernel,
        out_shape=(
            jax.ShapeDtypeStruct((1, count), I32),
            jax.ShapeDtypeStruct((count, 128), I32),
        ),
        in_specs=[scalars(), whole(), whole()],
        out_specs=(whole(), whole()),
        compiler_params=params(),
        cost_estimate=cost(COST['route']),
        name="route",
    )(place, ids, store)


def pack_kernel(e, row_ref, tok_ref, *refs):
    out_ref = refs[-1]
    hot = row_ref[...] == iota((ROWS, row_ref.shape[1]), 0) + e * ROWS
    out_ref[...] = jnp.dot(
        hot.astype(BF16), tok_ref[...], preferred_element_type=F32
    ).astype(BF16)


def pack(e, row, tokens, *earlier):
    return pl.pallas_call(
        functools.partial(pack_kernel, e),
        out_shape=jax.ShapeDtypeStruct((ROWS, tokens.shape[1]), BF16),
        in_specs=[whole()] * 2 + [pl.BlockSpec(memory_space=pl.ANY)] * len(earlier),
        out_specs=whole(),
        compiler_params=params(limit=24 * MIB),
        cost_estimate=cost(COST["pack"]),
        name="pack",
    )(row, tokens, *earlier)


def base_kernel(place_ref, tok_ref, w_ref, other_tok_ref, other_w_ref, *refs):
    total = jnp.zeros(refs[-1].shape[1:], F32)
    for t_ref, panel_ref in ((tok_ref, w_ref), (other_tok_ref, other_w_ref)):
        both = jnp.concatenate([panel_ref[0], panel_ref[1]], axis=1)
        total = total + jnp.dot(t_ref[...], both, preferred_element_type=F32)
    refs[-1][0] = total.astype(BF16)


def base(place, tokens, weight, other_tokens, other_weight, *earlier):
    count, width = tokens.shape
    rows = pl.BlockSpec((count, width), lambda i, place: (0, 0))
    columns = pl.BlockSpec((2, width, 128), lambda i, place: (0, 0, i * 2 + place[2]))
    return pl.pallas_call(
        base_kernel,
        grid_spec=pltpu.PrefetchScalarGridSpec(
            num_scalar_prefetch=1,
            grid=(NY,),
            in_specs=[rows, columns, rows, columns]
            + [pl.BlockSpec(memory_space=pl.ANY)] * len(earlier),
            out_specs=pl.BlockSpec((1, count, 256), lambda i, place: (i, 0, 0)),
        ),
        out_shape=jax.ShapeDtypeStruct((NY, count, 256), BF16),
        compiler_params=params("arbitrary"),
        cost_estimate=cost(COST["base"]),
        name="base",
    )(place, tokens, weight, other_tokens, other_weight, *earlier)


def adapter_of(skip, copies):
    row = iota((WIDE, 1), 0) - skip
    which = jnp.full((WIDE, 1), -1, I32)
    for a in range(LOCAL):
        which = jnp.where((row >= a * CAP) & (row < (a + 1) * CAP), a, which)
    return jnp.concatenate([which] * copies, axis=0)


def spans(blocks):
    return [(k, k * BLOCK // 16 * 16, k * BLOCK % 16) for k in range(len(blocks))]


def shrunk_rows(rows, panel, skip, copies):
    y = jnp.dot(
        rows,
        jnp.concatenate([panel[a] for a in range(LOCAL)], axis=1),
        preferred_element_type=F32,
    )
    which = adapter_of(skip, copies)
    kept = jnp.zeros((copies * WIDE, 128), F32)
    for a in range(LOCAL):
        kept = kept + jnp.where(which == a, y[:, a * 128 : (a + 1) * 128], 0.0)
    return kept


def shrink_blocks(xs, panels, blocks, total):
    for k, low, skip in spans(blocks):
        rows = jnp.concatenate([x[low : low + WIDE, :] for x in xs], axis=0)
        kept = shrunk_rows(rows, panels[k], skip, NX)
        for e in range(NX):
            total[e, low : low + WIDE, :] += kept[e * WIDE : (e + 1) * WIDE]


def shrink_near_kernel(place_ref, *refs):
    xs, panels = refs[:NX], refs[NX : NX + len(NEAR)]
    keep_ref, send_ref, total = refs[-3:]
    total[...] = jnp.zeros_like(total)
    shrink_blocks(xs, panels, NEAR, total)
    core = place_ref[2]
    keep_ref[...] = total[pl.ds(core * 2, 2)].astype(BF16)
    send_ref[...] = total[pl.ds(2 - core * 2, 2)].astype(BF16)


def shrink_near(place, xs, panels, *earlier):
    width = xs[0].shape[1]
    half = jax.ShapeDtypeStruct((2, NEAR_ROWS, 128), BF16)
    return pl.pallas_call(
        shrink_near_kernel,
        grid=(1,),
        out_shape=(half, half),
        in_specs=[scalars()]
        + [pl.BlockSpec((pl.Element(NEAR_ROWS), pl.Element(width)), lambda i: (0, 0))] * NX
        + [pl.BlockSpec((LOCAL, width, 128), lambda i: (0, 0, 0)) for w in panels]
        + [pl.BlockSpec(memory_space=pl.ANY)] * len(earlier),
        out_specs=(pl.BlockSpec(half.shape, lambda i: (0, 0, 0)),) * 2,
        scratch_shapes=[pltpu.VMEM((NX, NEAR_ROWS, 128), F32)],
        compiler_params=params("arbitrary", limit=32 * MIB),
        cost_estimate=cost(COST["shrink_near"]),
        name="shrink_near",
    )(place, *xs, *panels, *earlier)


def carve_kernel(*refs):
    xs, outs = refs[:NX], refs[NX:]
    for e in range(NX):
        outs[e // 2][e % 2] = xs[e][...]


def carve(xs):
    width = xs[0].shape[1]
    first = NEAR_ROWS + FAR_ROWS
    pair = jax.ShapeDtypeStruct((2, WIDE, width), BF16)
    return pl.pallas_call(
        carve_kernel,
        grid=(1,),
        out_shape=(pair, pair),
        in_specs=[pl.BlockSpec((pl.Element(WIDE), pl.Element(width)), lambda i: (first, 0))] * NX,
        out_specs=(pl.BlockSpec(pair.shape, lambda i: (0, 0, 0)),) * 2,
        compiler_params=params("arbitrary", limit=8 * MIB),
        cost_estimate=cost(COST["carve"]),
        name="carve",
    )(*xs)


def shrink_far_kernel(*refs):
    xs, panels = refs[:NX], refs[NX : NX + 2]
    out_ref, total = refs[-2:]
    total[...] = jnp.zeros_like(total)
    shrink_blocks(xs, panels, FAR, total)
    out_ref[...] = total[...].astype(BF16)


def shrink_far(xs, panels, *earlier):
    width = xs[0].shape[1]
    return pl.pallas_call(
        shrink_far_kernel,
        grid=(1,),
        out_shape=jax.ShapeDtypeStruct((NX, FAR_ROWS, 128), BF16),
        in_specs=[
            pl.BlockSpec((pl.Element(FAR_ROWS), pl.Element(width)), lambda i: (NEAR_ROWS, 0))
        ]
        * NX
        + [pl.BlockSpec((LOCAL, width, 128), lambda i: (0, 0, 0)) for w in panels]
        + [pl.BlockSpec(memory_space=pl.ANY)] * len(earlier),
        out_specs=pl.BlockSpec((NX, FAR_ROWS, 128), lambda i: (0, 0, 0)),
        scratch_shapes=[pltpu.VMEM((NX, FAR_ROWS, 128), F32)],
        compiler_params=params("arbitrary"),
        cost_estimate=cost(COST["shrink_far"]),
        name="shrink_far",
    )(*xs, *panels, *earlier)


def shrink_late_kernel(far_ref, from_low, from_high, low_ref, high_ref, _, out_ref):
    out_ref[:, :FAR_ROWS, :] = far_ref[...]
    for guest, panel, first in ((from_low, high_ref, 0), (from_high, low_ref, 2)):
        kept = shrunk_rows(jnp.concatenate([guest[0], guest[1]], axis=0), panel, 0, 2)
        for e in range(2):
            out_ref[first + e, FAR_ROWS:, :] = kept[e * WIDE : (e + 1) * WIDE].astype(BF16)


def shrink_late(far, guests, panels, earlier):
    width = guests[0].shape[2]
    return pl.pallas_call(
        shrink_late_kernel,
        grid=(1,),
        out_shape=jax.ShapeDtypeStruct((NX, LATE_ROWS, 128), BF16),
        in_specs=[pl.BlockSpec(a.shape, lambda i: (0, 0, 0)) for a in (far, *guests)]
        + [pl.BlockSpec((LOCAL, width, 128), lambda i: (0, 0, 0)) for w in panels]
        + [pl.BlockSpec(memory_space=pl.ANY)],
        out_specs=pl.BlockSpec((NX, LATE_ROWS, 128), lambda i: (0, 0, 0)),
        compiler_params=params("arbitrary"),
        cost_estimate=cost(COST["shrink_late"]),
        name="shrink_late",
    )(far, *guests, *panels, earlier)


def widen(up_ref, wide_up):
    for a in range(LOCAL):
        for c in range(2):
            wide_up[a * 128 + c * 64 : a * 128 + c * 64 + 64, c * 128 : (c + 1) * 128] = up_ref[
                a, c * 64 : (c + 1) * 64
            ]


def up_block(panel):
    return pl.BlockSpec((LOCAL, 128, 128), lambda i: (0, panel.shape[1] // 128 - 1, 0))


def expanded_rows(rows, wide_up, skip, copies):
    which = adapter_of(skip, copies)
    lhs = jnp.concatenate(
        [jnp.where(which == a, rows, jnp.zeros_like(rows)) for a in range(LOCAL)], axis=1
    )
    return jnp.dot(lhs, wide_up[...], preferred_element_type=F32)


def expand_near_kernel(place_ref, mine_ref, other_ref, *refs):
    ups, outs = refs[: len(NEAR)], refs[len(NEAR) : len(NEAR) + NX]
    wide_up, total, shrunk = refs[len(NEAR) + NX :]
    core = place_ref[2]
    shrunk[pl.ds(core * 2, 2)] = mine_ref[...]
    shrunk[pl.ds(2 - core * 2, 2)] = other_ref[...]
    wide_up[...] = jnp.zeros_like(wide_up)
    total[...] = jnp.zeros_like(total)
    for k, low, skip in spans(NEAR):
        widen(ups[k], wide_up)
        rows = jnp.concatenate([shrunk[e, low : low + WIDE] for e in range(NX)], axis=0)
        y = expanded_rows(rows, wide_up, skip, NX)
        for e in range(NX):
            total[e, low : low + WIDE, :] += y[e * WIDE : (e + 1) * WIDE]
    for e in range(NX):
        outs[e][...] = total[e].astype(BF16)


def expand_near(place, mine, other, panels):
    half = pl.BlockSpec(mine.shape, lambda i: (0, 0, 0))
    return pl.pallas_call(
        expand_near_kernel,
        grid=(1,),
        out_shape=[jax.ShapeDtypeStruct((NEAR_ROWS, 256), BF16)] * NX,
        in_specs=[scalars(), half, half] + [up_block(w) for w in panels],
        out_specs=[pl.BlockSpec((NEAR_ROWS, 256), lambda i: (0, 0))] * NX,
        scratch_shapes=[
            pltpu.VMEM((LOCAL * 128, 256), BF16),
            pltpu.VMEM((NX, NEAR_ROWS, 256), F32),
            pltpu.VMEM((NX, NEAR_ROWS, 128), BF16),
        ],
        compiler_params=params("arbitrary"),
        cost_estimate=cost(COST["expand_near"]),
        name="expand_near",
    )(place, mine, other, *panels)


def expand_late_kernel(mine_ref, other_ref, *refs):
    ups, outs = refs[: len(FAR)], refs[-3 - NX : -3]
    wides, total = refs[-3:-1], refs[-1]
    shrunk = (mine_ref[...].astype(F32) + other_ref[...].astype(F32)).astype(BF16)
    total[...] = jnp.zeros_like(total)
    for k, low, skip in spans(FAR):
        wide_up = wides[k]
        wide_up[...] = jnp.zeros_like(wide_up)
        widen(ups[k], wide_up)
        rows = jnp.concatenate([shrunk[e, low : low + WIDE] for e in range(NX)], axis=0)
        y = expanded_rows(rows, wide_up, skip, NX)
        for e in range(NX):
            total[e, low : low + WIDE, :] += y[e * WIDE : (e + 1) * WIDE]
    for wide_up, first in ((wides[1], 0), (wides[0], 2)):
        rows = jnp.concatenate([shrunk[first + e, FAR_ROWS:] for e in range(2)], axis=0)
        y = expanded_rows(rows, wide_up, 0, 2)
        for e in range(2):
            total[first + e, FAR_ROWS:, :] = y[e * WIDE : (e + 1) * WIDE]
    for e in range(NX):
        outs[e][...] = total[e].astype(BF16)


def expand_late(mine, other, panels, *earlier):
    full = pl.BlockSpec(mine.shape, lambda i: (0, 0, 0))
    return pl.pallas_call(
        expand_late_kernel,
        grid=(1,),
        out_shape=[jax.ShapeDtypeStruct((LATE_ROWS, 256), BF16)] * NX,
        in_specs=[full, full]
        + [up_block(w) for w in panels]
        + [pl.BlockSpec(memory_space=pl.ANY)] * len(earlier),
        out_specs=[pl.BlockSpec((LATE_ROWS, 256), lambda i: (0, 0))] * NX,
        scratch_shapes=[
            pltpu.VMEM((LOCAL * 128, 256), BF16),
            pltpu.VMEM((LOCAL * 128, 256), BF16),
            pltpu.VMEM((NX, LATE_ROWS, 256), F32),
        ],
        compiler_params=params("arbitrary"),
        cost_estimate=cost(COST["expand_late"]),
        name="expand_late",
    )(mine, other, *panels, *earlier)


def gather_kernel(col_ref, base_ref, *refs):
    deltas, out_ref, table = refs[:NX], refs[NX], refs[NX + 1]
    full = table.shape[0]
    filled = NX * NEAR_ROWS

    @pl.when(pl.program_id(0) == 0)
    def _():
        for e in range(NX):
            table[e * NEAR_ROWS : (e + 1) * NEAR_ROWS, :] = deltas[e][...]
        table[filled:, :] = jnp.zeros((full - filled, 256), BF16)

    place = iota((1, full), 1)
    slots = jnp.where(place < filled, place, -1)
    for e in range(1, NX):
        slots = jnp.where(
            (place >= e * NEAR_ROWS) & (place < filled), place + e * LATE_ROWS, slots
        )
    hot = (col_ref[:, :1] == slots).astype(BF16)
    total = jnp.dot(hot, table[...], preferred_element_type=F32)
    for part in range(NY):
        total = total + base_ref[part].astype(F32)
    out_ref[...] = total


def gather(col, parts, deltas):
    count = col.shape[0]
    step = 512
    return pl.pallas_call(
        gather_kernel,
        grid=(count // step,),
        out_shape=jax.ShapeDtypeStruct((count, 256), F32),
        in_specs=[
            pl.BlockSpec((step, 128), lambda i: (i, 0)),
            pl.BlockSpec((NY, step, 256), lambda i: (0, i, 0)),
        ]
        + [pl.BlockSpec(d.shape, lambda i: (0, 0)) for d in deltas],
        out_specs=pl.BlockSpec((step, 256), lambda i: (i, 0)),
        scratch_shapes=[pltpu.VMEM((1536, 256), BF16)],
        compiler_params=params("arbitrary"),
        cost_estimate=cost(COST["gather"]),
        name="gather",
    )(col, parts, *deltas)


def finish_kernel(col_ref, total_ref, *refs):
    deltas, guests, out_ref, both, table = refs[:NX], refs[NX : NX + 2], refs[-3], refs[-2], refs[-1]
    rows, full = col_ref.shape[0], table.shape[0]
    far = NX * FAR_ROWS

    @pl.when(pl.program_id(0) == 0)
    def _():
        for e in range(NX):
            table[e * FAR_ROWS : (e + 1) * FAR_ROWS, :] = deltas[e][:FAR_ROWS, :]
            low = far + e * WIDE
            table[low : low + WIDE, :] = guests[e // 2][e % 2]

    place = iota((1, full), 1)
    slots = place
    for e in range(NX):
        start = e * ROWS + NEAR_ROWS - e * FAR_ROWS
        slots = jnp.where((place >= e * FAR_ROWS) & (place < far), place + start, slots)
        low = far + e * WIDE
        start = e * ROWS + NEAR_ROWS + FAR_ROWS - low
        slots = jnp.where(place >= low, place + start, slots)
    hot = (col_ref[:, :1] == slots).astype(BF16)
    total = total_ref[...] + jnp.dot(hot, table[...], preferred_element_type=F32)
    both[pl.ds(0, rows, stride=2), :] = total[:, :128]
    both[pl.ds(1, rows, stride=2), :] = total[:, 128:]
    out_ref[...] = both[...].astype(BF16)


def finish(col, total, deltas, guests):
    count = col.shape[0]
    step = 512
    return pl.pallas_call(
        finish_kernel,
        grid=(count // step,),
        out_shape=jax.ShapeDtypeStruct((2 * count, 128), BF16),
        in_specs=[
            pl.BlockSpec((step, 128), lambda i: (i, 0)),
            pl.BlockSpec((step, 256), lambda i: (i, 0)),
        ]
        + [pl.BlockSpec(d.shape, lambda i: (0, 0)) for d in deltas]
        + [pl.BlockSpec(g.shape, lambda i: (0, 0, 0)) for g in guests],
        out_specs=pl.BlockSpec((2 * step, 128), lambda i: (i, 0)),
        scratch_shapes=[
            pltpu.VMEM((2 * step, 128), F32),
            pltpu.VMEM((NX * (FAR_ROWS + WIDE), 256), BF16),
        ],
        compiler_params=params("arbitrary", limit=24 * MIB),
        cost_estimate=cost(COST["finish"]),
        name="finish",
    )(col, total, *deltas, *guests)


def along_z(array, d):
    pairs = [(x * NZ + z, x * NZ + (z + d) % NZ) for x in range(NX) for z in range(NZ)]
    return lax.ppermute(array, "ad", pairs)


def along_x(array, d):
    pairs = [(x * NZ + z, (x + d) % NX * NZ + z) for x in range(NX) for z in range(NZ)]
    return lax.ppermute(array, "ad", pairs)


def with_core(array):
    return lax.ppermute(array, "tp", [(i, i ^ 1) for i in range(2 * NY)])


def with_even(array):
    return lax.ppermute(array, "tp", [(i, i ^ 2) for i in range(2 * NY)])


def with_odd(array):
    pairs = [(y * 2 + c, (NY - 1 - y) * 2 + c) for y in range(NY) for c in range(2)]
    return lax.ppermute(array, "tp", pairs)


def add(a, b):
    return (a.astype(F32) + b.astype(F32)).astype(BF16)


def home(deltas):
    return [deltas[0]] + [along_x(deltas[e], -e) for e in (1, 2, 3)]


def body(tokens, weight, down, up, ident, store):
    index, part = lax.axis_index("ad"), lax.axis_index("tp")
    place = jnp.stack([index >> 3, index & 7, part & 1]).astype(I32)
    columns = [[y * 2 + c for y in range(NY)] for c in range(2)]

    panels = jnp.concatenate([down, up.reshape(LOCAL, 128, 128)], axis=1)
    cw1, ccw1 = along_z(panels, 1), along_z(panels, -1)

    other_tokens = with_core(tokens)
    other_weight = with_core(weight)
    row, col = route(place, ident.reshape(1, -1), store.reshape(1, -1))
    packed = {e: pack(e, row, tokens) for e in (1, 3, 2)}
    moved = {e: along_x(packed[e], e) for e in (1, 3, 2)}
    xs = [pack(0, row, tokens)] + [moved[e] for e in (1, 2, 3)]
    chip_base = base(place, tokens, weight, other_tokens, other_weight, *packed.values())
    cw1, ccw1, chip_base = lax.optimization_barrier((cw1, ccw1, chip_base))
    parts = lax.all_to_all(chip_base, "tp", 0, 0, axis_index_groups=columns, tiled=True)

    cw2, ccw2 = along_z(cw1, 1), along_z(ccw1, -1)
    cw3, ccw3 = along_z(cw2, 1), along_z(ccw2, -1)
    upward, downward = carve(xs)
    guests = [along_z(upward, 1), along_z(downward, -1)]

    held = [panels, cw1, ccw1, cw2, ccw2]
    keep, send = shrink_near(place, xs, held, upward)
    near_chip = add(keep, with_core(send))
    near_pair = add(near_chip, with_even(near_chip))
    near_pair, cw3, ccw3 = lax.optimization_barrier((near_pair, cw3, ccw3))
    near_sum = add(near_pair, with_odd(near_pair))
    near = home(expand_near(place, near_sum, with_core(near_sum), held))

    late = shrink_far(xs, [cw3, ccw3], near_pair, parts)
    late = shrink_late(late, guests, [cw3, ccw3], near_sum)
    late = add(late, with_core(late))
    late = add(late, with_even(late))
    total = gather(col, parts, near)
    late = home(expand_late(late, with_odd(late), [cw3, ccw3], *near[1:]))
    opposite = [d[FAR_ROWS:] for d in late]
    back = [along_z(jnp.stack(opposite[:2]), -1), along_z(jnp.stack(opposite[2:]), 1)]

    out = finish(col, total, late, back)
    return out.reshape(tokens.shape[0], 2, 128)


def solution(mesh):
    return jax.shard_map(
        body,
        mesh=mesh,
        in_specs=(
            P("ad", "tp"),
            P(None, "tp", None),
            P("ad", "tp", None),
            P("ad", None, None, "tp"),
            P("ad", None),
            P(),
        ),
        out_specs=P("ad", None, "tp"),
        check_vma=False,
    )
```

```python
import functools

import jax
import jax.numpy as jnp
from jax import lax
from jax.experimental import pallas as pl
from jax.experimental.pallas import tpu as pltpu
from jax.sharding import PartitionSpec as P

F32 = jnp.float32
BF16 = jnp.bfloat16
I32 = jnp.int32

NX, NZ = 4, 8
NY = 4
LOCAL = 4
CAP = 18
BLOCK = LOCAL * CAP
WIDE = 80

NEAR = (0, 7, 1, 6, 2)
FAR = (5, 3)
OPPOSITE = 4
NEAR_ROWS = 368
FAR_ROWS = 144
ROWS = 592
LATE_ROWS = ROWS - NEAR_ROWS
START = {offset: k * BLOCK for k, offset in enumerate(NEAR)}
START.update({offset: NEAR_ROWS + k * BLOCK for k, offset in enumerate(FAR)})
START[OPPOSITE] = NEAR_ROWS + FAR_ROWS

MIB = 1024 * 1024
VMEM = 56 * MIB
COST = {
    "route": 3, "pack": 3, "base": 11, "carve": 1, "shrink_near": 3, "expand_near": 3,
    "shrink_far": 100, "shrink_late": 3, "expand_late": 30, "gather": 5, "finish": 5,
}
VMEM = 56 * 1024 * 1024


def iota(shape, dim):
    return lax.broadcasted_iota(I32, shape, dim)


def params(*semantics, limit=VMEM):
    if semantics:
        return pltpu.CompilerParams(vmem_limit_bytes=limit, dimension_semantics=semantics)
    return pltpu.CompilerParams(vmem_limit_bytes=limit)


def cost(micros):
    return pl.CostEstimate(
        flops=int(micros * 1.1e9), bytes_accessed=1000, transcendentals=0
    )


def whole():
    return pl.BlockSpec(memory_space=pltpu.VMEM)


def scalars():
    return pl.BlockSpec(memory_space=pltpu.SMEM)


def route_kernel(place_ref, ids_ref, store_ref, row_ref, col_ref):
    x, z = place_ref[0], place_ref[1]
    count = ids_ref.shape[1]
    ids = jnp.broadcast_to(ids_ref[...], (128, count))
    ids_down = ids.T
    store = jnp.broadcast_to(store_ref[...], (128, 128)).T
    for j in range(count // 128):
        mine = ids[:, j * 128 : (j + 1) * 128]
        placed = jnp.sum(
            jnp.where(mine == iota((128, 128), 0), store, 0), axis=0, keepdims=True
        )
        seen = (j + 1) * 128
        same = (ids_down[:seen] == mine[:1]) & (
            iota((seen, 128), 0) < iota((seen, 128), 1) + j * 128
        )
        ordinal = jnp.sum(same.astype(I32), axis=0, keepdims=True)
        owner = placed >> 2
        east = ((owner >> 3) - x) & 3
        north = ((owner & 7) - z) & 7
        start = jnp.zeros_like(owner)
        for offset, first in START.items():
            start = jnp.where(north == offset, first, start)
        row_ref[:, j * 128 : (j + 1) * 128] = (
            east * ROWS + start + (placed & 3) * CAP + ordinal
        )
    col_ref[...] = jnp.broadcast_to(row_ref[...], (128, count)).T


def route(place, ids, store):
    count = ids.shape[1]
    return pl.pallas_call(
        route_kernel,
        out_shape=(
            jax.ShapeDtypeStruct((1, count), I32),
            jax.ShapeDtypeStruct((count, 128), I32),
        ),
        in_specs=[scalars(), whole(), whole()],
        out_specs=(whole(), whole()),
        compiler_params=params(),
        cost_estimate=cost(COST['route']),
        name="route",
    )(place, ids, store)


def pack_kernel(e, row_ref, tok_ref, *refs):
    out_ref = refs[-1]
    hot = row_ref[...] == iota((ROWS, row_ref.shape[1]), 0) + e * ROWS
    out_ref[...] = jnp.dot(
        hot.astype(BF16), tok_ref[...], preferred_element_type=F32
    ).astype(BF16)


def pack(e, row, tokens, *earlier):
    return pl.pallas_call(
        functools.partial(pack_kernel, e),
        out_shape=jax.ShapeDtypeStruct((ROWS, tokens.shape[1]), BF16),
        in_specs=[whole()] * 2 + [pl.BlockSpec(memory_space=pl.ANY)] * len(earlier),
        out_specs=whole(),
        compiler_params=params(limit=24 * MIB),
        cost_estimate=cost(COST["pack"]),
        name="pack",
    )(row, tokens, *earlier)


def base_kernel(place_ref, tok_ref, w_ref, other_tok_ref, other_w_ref, *refs):
    total = jnp.zeros(refs[-1].shape[1:], F32)
    for t_ref, panel_ref in ((tok_ref, w_ref), (other_tok_ref, other_w_ref)):
        both = jnp.concatenate([panel_ref[0], panel_ref[1]], axis=1)
        total = total + jnp.dot(t_ref[...], both, preferred_element_type=F32)
    refs[-1][0] = total.astype(BF16)


def base(place, tokens, weight, other_tokens, other_weight, *earlier):
    count, width = tokens.shape
    rows = pl.BlockSpec((count, width), lambda i, place: (0, 0))
    columns = pl.BlockSpec((2, width, 128), lambda i, place: (0, 0, i * 2 + place[2]))
    return pl.pallas_call(
        base_kernel,
        grid_spec=pltpu.PrefetchScalarGridSpec(
            num_scalar_prefetch=1,
            grid=(NY,),
            in_specs=[rows, columns, rows, columns]
            + [pl.BlockSpec(memory_space=pl.ANY)] * len(earlier),
            out_specs=pl.BlockSpec((1, count, 256), lambda i, place: (i, 0, 0)),
        ),
        out_shape=jax.ShapeDtypeStruct((NY, count, 256), BF16),
        compiler_params=params("arbitrary"),
        cost_estimate=cost(COST["base"]),
        name="base",
    )(place, tokens, weight, other_tokens, other_weight, *earlier)


def adapter_of(skip, copies):
    row = iota((WIDE, 1), 0) - skip
    which = jnp.full((WIDE, 1), -1, I32)
    for a in range(LOCAL):
        which = jnp.where((row >= a * CAP) & (row < (a + 1) * CAP), a, which)
    return jnp.concatenate([which] * copies, axis=0)


def spans(blocks):
    return [(k, k * BLOCK // 16 * 16, k * BLOCK % 16) for k in range(len(blocks))]


def shrunk_rows(rows, panel, skip, copies):
    y = jnp.dot(
        rows,
        jnp.concatenate([panel[a] for a in range(LOCAL)], axis=1),
        preferred_element_type=F32,
    )
    which = adapter_of(skip, copies)
    kept = jnp.zeros((copies * WIDE, 128), F32)
    for a in range(LOCAL):
        kept = kept + jnp.where(which == a, y[:, a * 128 : (a + 1) * 128], 0.0)
    return kept


def shrink_blocks(xs, panels, blocks, total):
    for k, low, skip in spans(blocks):
        rows = jnp.concatenate([x[low : low + WIDE, :] for x in xs], axis=0)
        kept = shrunk_rows(rows, panels[k], skip, NX)
        for e in range(NX):
            total[e, low : low + WIDE, :] += kept[e * WIDE : (e + 1) * WIDE]


def shrink_near_kernel(place_ref, *refs):
    xs, panels = refs[:NX], refs[NX : NX + len(NEAR)]
    keep_ref, send_ref, total = refs[-3:]
    total[...] = jnp.zeros_like(total)
    shrink_blocks(xs, panels, NEAR, total)
    core = place_ref[2]
    keep_ref[...] = total[pl.ds(core * 2, 2)].astype(BF16)
    send_ref[...] = total[pl.ds(2 - core * 2, 2)].astype(BF16)


def shrink_near(place, xs, panels, *earlier):
    width = xs[0].shape[1]
    half = jax.ShapeDtypeStruct((2, NEAR_ROWS, 128), BF16)
    return pl.pallas_call(
        shrink_near_kernel,
        grid=(1,),
        out_shape=(half, half),
        in_specs=[scalars()]
        + [pl.BlockSpec((pl.Element(NEAR_ROWS), pl.Element(width)), lambda i: (0, 0))] * NX
        + [pl.BlockSpec((LOCAL, width, 128), lambda i: (0, 0, 0)) for w in panels]
        + [pl.BlockSpec(memory_space=pl.ANY)] * len(earlier),
        out_specs=(pl.BlockSpec(half.shape, lambda i: (0, 0, 0)),) * 2,
        scratch_shapes=[pltpu.VMEM((NX, NEAR_ROWS, 128), F32)],
        compiler_params=params("arbitrary", limit=32 * MIB),
        cost_estimate=cost(COST["shrink_near"]),
        name="shrink_near",
    )(place, *xs, *panels, *earlier)


def carve_kernel(*refs):
    xs, outs = refs[:NX], refs[NX:]
    for e in range(NX):
        outs[e // 2][e % 2] = xs[e][...]


def carve(xs):
    width = xs[0].shape[1]
    first = NEAR_ROWS + FAR_ROWS
    pair = jax.ShapeDtypeStruct((2, WIDE, width), BF16)
    return pl.pallas_call(
        carve_kernel,
        grid=(1,),
        out_shape=(pair, pair),
        in_specs=[pl.BlockSpec((pl.Element(WIDE), pl.Element(width)), lambda i: (first, 0))] * NX,
        out_specs=(pl.BlockSpec(pair.shape, lambda i: (0, 0, 0)),) * 2,
        compiler_params=params("arbitrary", limit=8 * MIB),
        cost_estimate=cost(COST["carve"]),
        name="carve",
    )(*xs)


def shrink_far_kernel(*refs):
    xs, panels = refs[:NX], refs[NX : NX + 2]
    out_ref, total = refs[-2:]
    total[...] = jnp.zeros_like(total)
    shrink_blocks(xs, panels, FAR, total)
    out_ref[...] = total[...].astype(BF16)


def shrink_far(xs, panels, *earlier):
    width = xs[0].shape[1]
    return pl.pallas_call(
        shrink_far_kernel,
        grid=(1,),
        out_shape=jax.ShapeDtypeStruct((NX, FAR_ROWS, 128), BF16),
        in_specs=[
            pl.BlockSpec((pl.Element(FAR_ROWS), pl.Element(width)), lambda i: (NEAR_ROWS, 0))
        ]
        * NX
        + [pl.BlockSpec((LOCAL, width, 128), lambda i: (0, 0, 0)) for w in panels]
        + [pl.BlockSpec(memory_space=pl.ANY)] * len(earlier),
        out_specs=pl.BlockSpec((NX, FAR_ROWS, 128), lambda i: (0, 0, 0)),
        scratch_shapes=[pltpu.VMEM((NX, FAR_ROWS, 128), F32)],
        compiler_params=params("arbitrary", limit=16 * MIB),
        cost_estimate=cost(COST["shrink_far"]),
        name="shrink_far",
    )(*xs, *panels, *earlier)


def shrink_late_kernel(far_ref, from_low, from_high, low_ref, high_ref, _, out_ref):
    out_ref[:, :FAR_ROWS, :] = far_ref[...]
    for guest, panel, first in ((from_low, high_ref, 0), (from_high, low_ref, 2)):
        kept = shrunk_rows(jnp.concatenate([guest[0], guest[1]], axis=0), panel, 0, 2)
        for e in range(2):
            out_ref[first + e, FAR_ROWS:, :] = kept[e * WIDE : (e + 1) * WIDE].astype(BF16)


def shrink_late(far, guests, panels, earlier):
    width = guests[0].shape[2]
    return pl.pallas_call(
        shrink_late_kernel,
        grid=(1,),
        out_shape=jax.ShapeDtypeStruct((NX, LATE_ROWS, 128), BF16),
        in_specs=[pl.BlockSpec(a.shape, lambda i: (0, 0, 0)) for a in (far, *guests)]
        + [pl.BlockSpec((LOCAL, width, 128), lambda i: (0, 0, 0)) for w in panels]
        + [pl.BlockSpec(memory_space=pl.ANY)],
        out_specs=pl.BlockSpec((NX, LATE_ROWS, 128), lambda i: (0, 0, 0)),
        compiler_params=params("arbitrary", limit=16 * MIB),
        cost_estimate=cost(COST["shrink_late"]),
        name="shrink_late",
    )(far, *guests, *panels, earlier)


def widen(up_ref, wide_up):
    for a in range(LOCAL):
        for c in range(2):
            wide_up[a * 128 + c * 64 : a * 128 + c * 64 + 64, c * 128 : (c + 1) * 128] = up_ref[
                a, c * 64 : (c + 1) * 64
            ]


def up_block(panel):
    return pl.BlockSpec((LOCAL, 128, 128), lambda i: (0, panel.shape[1] // 128 - 1, 0))


def expanded_rows(rows, wide_up, skip, copies):
    which = adapter_of(skip, copies)
    lhs = jnp.concatenate(
        [jnp.where(which == a, rows, jnp.zeros_like(rows)) for a in range(LOCAL)], axis=1
    )
    return jnp.dot(lhs, wide_up[...], preferred_element_type=F32)


def expand_near_kernel(place_ref, mine_ref, other_ref, *refs):
    ups, outs = refs[: len(NEAR)], refs[len(NEAR) : len(NEAR) + NX]
    wide_up, total, shrunk = refs[len(NEAR) + NX :]
    core = place_ref[2]
    shrunk[pl.ds(core * 2, 2)] = mine_ref[...]
    shrunk[pl.ds(2 - core * 2, 2)] = other_ref[...]
    wide_up[...] = jnp.zeros_like(wide_up)
    total[...] = jnp.zeros_like(total)
    for k, low, skip in spans(NEAR):
        widen(ups[k], wide_up)
        rows = jnp.concatenate([shrunk[e, low : low + WIDE] for e in range(NX)], axis=0)
        y = expanded_rows(rows, wide_up, skip, NX)
        for e in range(NX):
            total[e, low : low + WIDE, :] += y[e * WIDE : (e + 1) * WIDE]
    for e in range(NX):
        outs[e][...] = total[e].astype(BF16)


def expand_near(place, mine, other, panels):
    half = pl.BlockSpec(mine.shape, lambda i: (0, 0, 0))
    return pl.pallas_call(
        expand_near_kernel,
        grid=(1,),
        out_shape=[jax.ShapeDtypeStruct((NEAR_ROWS, 256), BF16)] * NX,
        in_specs=[scalars(), half, half] + [up_block(w) for w in panels],
        out_specs=[pl.BlockSpec((NEAR_ROWS, 256), lambda i: (0, 0))] * NX,
        scratch_shapes=[
            pltpu.VMEM((LOCAL * 128, 256), BF16),
            pltpu.VMEM((NX, NEAR_ROWS, 256), F32),
            pltpu.VMEM((NX, NEAR_ROWS, 128), BF16),
        ],
        compiler_params=params("arbitrary", limit=24 * MIB),
        cost_estimate=cost(COST["expand_near"]),
        name="expand_near",
    )(place, mine, other, *panels)


def expand_late_kernel(mine_ref, other_ref, *refs):
    ups, outs = refs[: len(FAR)], refs[-3 - NX : -3]
    wides, total = refs[-3:-1], refs[-1]
    shrunk = (mine_ref[...].astype(F32) + other_ref[...].astype(F32)).astype(BF16)
    total[...] = jnp.zeros_like(total)
    for k, low, skip in spans(FAR):
        wide_up = wides[k]
        wide_up[...] = jnp.zeros_like(wide_up)
        widen(ups[k], wide_up)
        rows = jnp.concatenate([shrunk[e, low : low + WIDE] for e in range(NX)], axis=0)
        y = expanded_rows(rows, wide_up, skip, NX)
        for e in range(NX):
            total[e, low : low + WIDE, :] += y[e * WIDE : (e + 1) * WIDE]
    for wide_up, first in ((wides[1], 0), (wides[0], 2)):
        rows = jnp.concatenate([shrunk[first + e, FAR_ROWS:] for e in range(2)], axis=0)
        y = expanded_rows(rows, wide_up, 0, 2)
        for e in range(2):
            total[first + e, FAR_ROWS:, :] = y[e * WIDE : (e + 1) * WIDE]
    for e in range(NX):
        outs[e][...] = total[e].astype(BF16)


def expand_late(mine, other, panels, *earlier):
    full = pl.BlockSpec(mine.shape, lambda i: (0, 0, 0))
    return pl.pallas_call(
        expand_late_kernel,
        grid=(1,),
        out_shape=[jax.ShapeDtypeStruct((LATE_ROWS, 256), BF16)] * NX,
        in_specs=[full, full]
        + [up_block(w) for w in panels]
        + [pl.BlockSpec(memory_space=pl.ANY)] * len(earlier),
        out_specs=[pl.BlockSpec((LATE_ROWS, 256), lambda i: (0, 0))] * NX,
        scratch_shapes=[
            pltpu.VMEM((LOCAL * 128, 256), BF16),
            pltpu.VMEM((LOCAL * 128, 256), BF16),
            pltpu.VMEM((NX, LATE_ROWS, 256), F32),
        ],
        compiler_params=params("arbitrary", limit=24 * MIB),
        cost_estimate=cost(COST["expand_late"]),
        name="expand_late",
    )(mine, other, *panels, *earlier)


def gather_kernel(col_ref, base_ref, *refs):
    deltas, out_ref, table = refs[:NX], refs[NX], refs[NX + 1]
    full = table.shape[0]
    filled = NX * NEAR_ROWS

    @pl.when(pl.program_id(0) == 0)
    def _():
        for e in range(NX):
            table[e * NEAR_ROWS : (e + 1) * NEAR_ROWS, :] = deltas[e][...]
        table[filled:, :] = jnp.zeros((full - filled, 256), BF16)

    place = iota((1, full), 1)
    slots = jnp.where(place < filled, place, -1)
    for e in range(1, NX):
        slots = jnp.where(
            (place >= e * NEAR_ROWS) & (place < filled), place + e * LATE_ROWS, slots
        )
    hot = (col_ref[:, :1] == slots).astype(BF16)
    total = jnp.dot(hot, table[...], preferred_element_type=F32)
    for part in range(NY):
        total = total + base_ref[part].astype(F32)
    out_ref[...] = total


def gather(col, parts, deltas):
    count = col.shape[0]
    step = 512
    return pl.pallas_call(
        gather_kernel,
        grid=(count // step,),
        out_shape=jax.ShapeDtypeStruct((count, 256), F32),
        in_specs=[
            pl.BlockSpec((step, 128), lambda i: (i, 0)),
            pl.BlockSpec((NY, step, 256), lambda i: (0, i, 0)),
        ]
        + [pl.BlockSpec(d.shape, lambda i: (0, 0)) for d in deltas],
        out_specs=pl.BlockSpec((step, 256), lambda i: (i, 0)),
        scratch_shapes=[pltpu.VMEM((1536, 256), BF16)],
        compiler_params=params("arbitrary"),
        cost_estimate=cost(COST["gather"]),
        name="gather",
    )(col, parts, *deltas)


def finish_kernel(col_ref, total_ref, *refs):
    deltas, guests, out_ref, both, table = refs[:NX], refs[NX : NX + 2], refs[-3], refs[-2], refs[-1]
    rows, full = col_ref.shape[0], table.shape[0]
    far = NX * FAR_ROWS

    @pl.when(pl.program_id(0) == 0)
    def _():
        for e in range(NX):
            table[e * FAR_ROWS : (e + 1) * FAR_ROWS, :] = deltas[e][:FAR_ROWS, :]
            low = far + e * WIDE
            table[low : low + WIDE, :] = guests[e // 2][e % 2]

    place = iota((1, full), 1)
    slots = place
    for e in range(NX):
        start = e * ROWS + NEAR_ROWS - e * FAR_ROWS
        slots = jnp.where((place >= e * FAR_ROWS) & (place < far), place + start, slots)
        low = far + e * WIDE
        start = e * ROWS + NEAR_ROWS + FAR_ROWS - low
        slots = jnp.where(place >= low, place + start, slots)
    hot = (col_ref[:, :1] == slots).astype(BF16)
    total = total_ref[...] + jnp.dot(hot, table[...], preferred_element_type=F32)
    both[pl.ds(0, rows, stride=2), :] = total[:, :128]
    both[pl.ds(1, rows, stride=2), :] = total[:, 128:]
    out_ref[...] = both[...].astype(BF16)


def finish(col, total, deltas, guests):
    count = col.shape[0]
    step = 512
    return pl.pallas_call(
        finish_kernel,
        grid=(count // step,),
        out_shape=jax.ShapeDtypeStruct((2 * count, 128), BF16),
        in_specs=[
            pl.BlockSpec((step, 128), lambda i: (i, 0)),
            pl.BlockSpec((step, 256), lambda i: (i, 0)),
        ]
        + [pl.BlockSpec(d.shape, lambda i: (0, 0)) for d in deltas]
        + [pl.BlockSpec(g.shape, lambda i: (0, 0, 0)) for g in guests],
        out_specs=pl.BlockSpec((2 * step, 128), lambda i: (i, 0)),
        scratch_shapes=[
            pltpu.VMEM((2 * step, 128), F32),
            pltpu.VMEM((NX * (FAR_ROWS + WIDE), 256), BF16),
        ],
        compiler_params=params("arbitrary", limit=24 * MIB),
        cost_estimate=cost(COST["finish"]),
        name="finish",
    )(col, total, *deltas, *guests)


def along_z(array, d):
    pairs = [(x * NZ + z, x * NZ + (z + d) % NZ) for x in range(NX) for z in range(NZ)]
    return lax.ppermute(array, "ad", pairs)


def along_x(array, d):
    pairs = [(x * NZ + z, (x + d) % NX * NZ + z) for x in range(NX) for z in range(NZ)]
    return lax.ppermute(array, "ad", pairs)


def with_core(array):
    return lax.ppermute(array, "tp", [(i, i ^ 1) for i in range(2 * NY)])


def with_even(array):
    return lax.ppermute(array, "tp", [(i, i ^ 2) for i in range(2 * NY)])


def with_odd(array):
    pairs = [(y * 2 + c, (NY - 1 - y) * 2 + c) for y in range(NY) for c in range(2)]
    return lax.ppermute(array, "tp", pairs)


def add(a, b):
    return (a.astype(F32) + b.astype(F32)).astype(BF16)


def home(deltas):
    return [deltas[0]] + [along_x(deltas[e], -e) for e in (1, 2, 3)]


def body(tokens, weight, down, up, ident, store):
    index, part = lax.axis_index("ad"), lax.axis_index("tp")
    place = jnp.stack([index >> 3, index & 7, part & 1]).astype(I32)
    columns = [[y * 2 + c for y in range(NY)] for c in range(2)]

    panels = jnp.concatenate([down, up.reshape(LOCAL, 128, 128)], axis=1)
    cw1, ccw1 = along_z(panels, 1), along_z(panels, -1)

    other_tokens = with_core(tokens)
    other_weight = with_core(weight)
    row, col = route(place, ident.reshape(1, -1), store.reshape(1, -1))
    packed = {e: pack(e, row, tokens) for e in (1, 3, 2)}
    moved = {e: along_x(packed[e], e) for e in (1, 3, 2)}
    xs = [pack(0, row, tokens)] + [moved[e] for e in (1, 2, 3)]
    chip_base = base(place, tokens, weight, other_tokens, other_weight, *packed.values())
    cw1, ccw1, chip_base = lax.optimization_barrier((cw1, ccw1, chip_base))
    parts = lax.all_to_all(chip_base, "tp", 0, 0, axis_index_groups=columns, tiled=True)

    cw2, ccw2 = along_z(cw1, 1), along_z(ccw1, -1)
    cw3, ccw3 = along_z(cw2, 1), along_z(ccw2, -1)
    upward, downward = carve(xs)
    guests = [along_z(upward, 1), along_z(downward, -1)]

    held = [panels, cw1, ccw1, cw2, ccw2]
    keep, send = shrink_near(place, xs, held, upward)
    near_chip = add(keep, with_core(send))
    near_pair = add(near_chip, with_even(near_chip))
    near_sum = add(near_pair, with_odd(near_pair))
    near = home(expand_near(place, near_sum, with_core(near_sum), held))

    late = shrink_far(xs, [cw3, ccw3], near_chip, parts)
    late = shrink_late(late, guests, [cw3, ccw3], near_pair)
    late = add(late, with_core(late))
    late = add(late, with_even(late))
    total = gather(col, parts, near)
    late = home(expand_late(late, with_odd(late), [cw3, ccw3], *near[1:]))
    opposite = [d[FAR_ROWS:] for d in late]
    back = [along_z(jnp.stack(opposite[:2]), -1), along_z(jnp.stack(opposite[2:]), 1)]

    out = finish(col, total, late, back)
    return out.reshape(tokens.shape[0], 2, 128)


def solution(mesh):
    return jax.shard_map(
        body,
        mesh=mesh,
        in_specs=(
            P("ad", "tp"),
            P(None, "tp", None),
            P("ad", "tp", None),
            P("ad", None, None, "tp"),
            P("ad", None),
            P(),
        ),
        out_specs=P("ad", None, "tp"),
        check_vma=False,
    )
```
